32 devices in a mesh: clus: 16 (over z, x, core), coef: 2 (over y).
Axes of the slice: x: 2, y: 2, z: 4, core: 2. Of those that a mesh axis runs over, the one named last changes fastest.
Arguments:
- density: bfloat16 [256, 128, 256], P('clus', 'coef'), may hold values from -6 to 6
- near_list: int32 [256, 9], P('clus'), may hold values from 0 to 255, as said below
- far_list: int32 [32, 27], P('clus'), may hold values from 0 to 31
- near_blocks: bfloat16 [256, 9, 128, 128], P('clus', None, 'coef'), may hold values from -0.1875 to 0.1875
- basis: bfloat16 [256, 128, 64], P('clus', 'coef'), may hold values from -0.5 to 0.5
- transfer: bfloat16 [256, 64, 64], P('clus'), may hold values from -0.25 to 0.25
- coupling: bfloat16 [32, 27, 64, 64], P('clus', None, None, 'coef'), may hold values from -0.15625 to 0.15625
Outputs:
- first: bfloat16 [256, 128, 256], P('clus', 'coef')
- second: bfloat16 [256, 128, 256], P('clus', 'coef')
The draws below stay inside these ranges and needn't reach their ends.
Inputs may be any that keep to these rules, and one draw needn't show every extreme that they name: near_list[i, 0] is i itself; every entry differs from its row's cluster i by at most 4, and entries i + 4 and i - 4 appear wherever they lie in range.
All inputs are finite; a program needn't handle non-finite values.
Results may differ from the reference program's by a relative error of at most 0.014.
Values may be sent and summed in bfloat16 or wider, within the bound.
A program may use at most 64 MiB of HBM per device.

```python
import jax
import jax.numpy as jnp
from jax import lax

PANEL = 128
RANK = 64
NRHS = 256
CHILD = 8
NEAR_K = 9
FAR_K = 27
NWIN = 4
CLUSTERS = 256
PARENTS = 32


def draw_near_list(key, part):
    rows = jnp.arange(CLUSTERS, dtype=jnp.int32)[:, None]
    shifts = jax.random.randint(key, (CLUSTERS, NEAR_K), -NWIN, NWIN + 1, dtype=jnp.int32)
    column = jnp.arange(NEAR_K, dtype=jnp.int32)[None, :]
    shifts = jnp.where(column == 0, 0, jnp.where(column == 1, NWIN, jnp.where(column == 2, -NWIN, shifts)))
    return jnp.clip(rows + shifts, 0, CLUSTERS - 1).astype(jnp.int32)


def place_ends(array, key, least, top_value):
    longest = array.shape.index(max(array.shape))
    spots = []
    for shift in (0, 1):
        where = [jax.random.randint(jax.random.fold_in(key, axis), (), 0, length) for axis, length in enumerate(array.shape)]
        where[longest] = (where[longest] + shift) % array.shape[longest]
        spots.append(tuple(where))
    return array.at[spots[0]].set(least).at[spots[1]].set(top_value)


def shard_levels(rng, shape, shards, low, high):
    factor_of, own = 1.0, jax.random.fold_in(rng, 6)
    for dim, parts in shards:
        draws = jnp.exp(jax.random.uniform(jax.random.fold_in(own, dim), (parts,), jnp.float32, low / len(shards), high / len(shards)))
        factor_of = factor_of * jnp.repeat(draws, shape[dim] // parts).reshape([-1 if axis == dim else 1 for axis in range(len(shape))])
    return factor_of


def bell_draw(stream_key, shape, spread, reach, pieces=(), held_as=jnp.bfloat16):
    array = spread * jax.random.normal(stream_key, shape, jnp.float32)
    if pieces:
        array = array * shard_levels(stream_key, shape, pieces, -0.22, 0.18)
    return jnp.clip(array, -reach, reach).astype(held_as)


def setup_inputs(seed: int = 0) -> dict:
    splits = jax.random.split(jax.random.key(seed), 8)
    return {
        "density": bell_draw(splits[0], (CLUSTERS, PANEL, NRHS), 1.0, 6.0, ((0, 16), (1, 2))),
        "near_list": draw_near_list(jax.random.fold_in(splits[7], 71), 0),
        "far_list": place_ends(jax.random.randint(splits[2], (PARENTS, FAR_K), 0, PARENTS), jax.random.fold_in(splits[2], 1), 0, PARENTS - 1).astype(jnp.int32),
        "near_blocks": bell_draw(splits[3], (CLUSTERS, NEAR_K, PANEL, PANEL), (NEAR_K * PANEL) ** -0.5, 0.1875, ((0, 16), (2, 2))),
        "basis": bell_draw(splits[4], (CLUSTERS, PANEL, RANK), PANEL ** -0.5, 0.5, ((0, 16), (1, 2))),
        "transfer": bell_draw(splits[5], (CLUSTERS, RANK, RANK), (CHILD * RANK) ** -0.5, 0.25, ((0, 16),)),
        "coupling": bell_draw(splits[6], (PARENTS, FAR_K, RANK, RANK), (FAR_K * RANK) ** -0.5, 0.15625, ((0, 16), (3, 2))),
    }


def apply_operator(values, near_list, far_list, near_blocks, basis, transfer, coupling):
    clusters = values.shape[0]
    parents = clusters // CHILD
    highest = lax.Precision.HIGHEST
    wide = values.astype(jnp.float32)
    base = basis.astype(jnp.float32)
    coeffs = jnp.einsum('ins,inr->isr', base, wide, precision=highest)
    grouped = transfer.astype(jnp.float32).reshape(parents, CHILD, RANK, RANK)
    parent_coef = jnp.einsum('pcsq,pcsr->pqr', grouped, coeffs.reshape(parents, CHILD, RANK, NRHS), precision=highest).astype(jnp.bfloat16)
    picked = jnp.take(parent_coef, far_list.reshape(-1), axis=0).reshape(parents, FAR_K, RANK, NRHS).astype(jnp.float32)
    coupled = jnp.einsum('pkaq,pkqr->par', coupling.astype(jnp.float32), picked, precision=highest).astype(jnp.bfloat16)
    lower = jnp.einsum('pcsq,pqr->pcsr', grouped, coupled.astype(jnp.float32), precision=highest).astype(jnp.bfloat16)
    lower = lower.reshape(clusters, RANK, NRHS).astype(jnp.float32)
    total = jnp.einsum('ins,isr->inr', base, lower, precision=highest)
    for column in range(NEAR_K):
        rows = jnp.take(values, near_list[:, column], axis=0).astype(jnp.float32)
        total = total + jnp.einsum('imn,inr->imr', near_blocks[:, column].astype(jnp.float32), rows, precision=highest)
    return total.astype(jnp.bfloat16)


def reference(density, near_list, far_list, near_blocks, basis, transfer, coupling):
    first = apply_operator(density, near_list, far_list, near_blocks, basis, transfer, coupling)
    second = apply_operator(first, near_list, far_list, near_blocks, basis, transfer, coupling)
    return (first, second)
```

```python
import functools

import jax
import jax.numpy as jnp
from jax import lax
from jax.experimental import pallas as pl
from jax.experimental.pallas import tpu as pltpu
from jax.sharding import PartitionSpec as P

CHILD = 8
NWIN = 4
MESH = pl.DeviceIdType.MESH
F32 = jnp.float32
BF16 = jnp.bfloat16


def kernel(
    nc, nk,
    density, near_list, far_list, nb_hbm, basis, transfer, coupling_hbm,
    first, second,
    nb, coupling, clhs, grow, ext_a, ext_b, rs_send, rs_recv, pc_a, pc_b, cp_send, cp_recv, far,
    load_sem, own_sem, y_send, y_recv, h_send, h_recv, rs_ssem, rs_rsem,
    z_ssem, z_rsem, x_ssem, x_rsem, c_ssem, c_rsem, cp_ssem, cp_rsem,
):
    leaves, rows, vectors = density.shape
    parents = leaves // CHILD
    near_k = nb.shape[1]
    far_k = coupling.shape[1]
    share = coupling.shape[3]
    rank = grow.shape[2]
    outer = nc // 4
    chunks = leaves // NWIN
    clus = lax.axis_index("clus")
    coef = lax.axis_index("coef")
    core = lax.rem(clus, 2)
    xpos = lax.rem(clus // 2, 2)
    zpos = clus // 4
    ext = (ext_a, ext_b)
    pc = (pc_a, pc_b)
    my_rows = pl.ds(pl.multiple_of(coef * rows, rows), rows)

    loads = [
        pltpu.make_async_copy(nb_hbm, nb, load_sem.at[0]),
        pltpu.make_async_copy(coupling_hbm, coupling, load_sem.at[1]),
    ]
    for load in loads:
        load.start()

    def at_coef(d):
        return lax.rem(coef + d, nk)

    def at_clus(z, x, c):
        return (z * 2 + x) * 2 + c

    def ring_z(e):
        return lax.rem(zpos + e, outer)

    barrier = pltpu.get_barrier_semaphore()

    def greet(c, k):
        pl.semaphore_signal(barrier, inc=1, device_id=(c, k), device_id_type=MESH)

    for d in range(1, nk):
        greet(clus, at_coef(d))
    for e in range(1, outer):
        greet(at_clus(ring_z(e), xpos, core), coef)
    greet(at_clus(zpos, 1 - xpos, core), coef)
    greet(at_clus(zpos, xpos, 1 - core), coef)

    @pl.when(clus > 0)
    def _():
        greet(clus - 1, coef)

    @pl.when(clus < nc - 1)
    def _():
        greet(clus + 1, coef)

    pl.semaphore_wait(
        barrier, nk + outer + jnp.minimum(clus, 1) + jnp.minimum(nc - 1 - clus, 1)
    )

    def remote(src, dst, ssem, rsem, c, k):
        return pltpu.make_async_remote_copy(
            src_ref=src, dst_ref=dst, send_sem=ssem, recv_sem=rsem,
            device_id=(c, k), device_id_type=MESH,
        )

    def y_copy(a, values, d, chunk):
        start = chunk * NWIN
        return remote(
            values.at[pl.ds(start, NWIN)],
            ext[a].at[pl.ds(NWIN + start, NWIN), my_rows],
            y_send.at[a, d, chunk], y_recv.at[a, d, chunk], clus, at_coef(d),
        )

    def halo_copy(a, values, d, up):
        lo = leaves - NWIN if up else 0
        dst_lo = 0 if up else NWIN + leaves
        owner = lax.rem(coef + nk - d, nk)
        span = pl.ds(pl.multiple_of(owner * rows, rows), rows)
        src = values.at[pl.ds(lo, NWIN)] if d == 0 else ext[a].at[pl.ds(NWIN + lo, NWIN), span]
        side = 1 if up else 0
        return remote(
            src, ext[a].at[pl.ds(dst_lo, NWIN), span],
            h_send.at[a, side, d], h_recv.at[a, side, d], clus + (1 if up else -1), coef,
        )

    def halo_start(a, values, d, up):
        @pl.when((clus < nc - 1) if up else (clus > 0))
        def _():
            halo_copy(a, values, d, up).start()

    def halo_wait_send(a, values, d, up):
        @pl.when((clus < nc - 1) if up else (clus > 0))
        def _():
            halo_copy(a, values, d, up).wait_send()

    def halo_wait_recv(a, values, d, up):
        @pl.when((clus > 0) if up else (clus < nc - 1))
        def _():
            halo_copy(a, values, d, up).wait_recv()

    def piece(a, c):
        return pc[a].at[pl.ds(c * parents, parents)]

    def z_copy(a, e):
        return remote(
            piece(a, clus), piece(a, clus), z_ssem.at[a, e], z_rsem.at[a, e],
            at_clus(ring_z(e), xpos, core), coef,
        )

    def x_copy(a, e):
        at = at_clus(ring_z(e), xpos, core)
        return remote(
            piece(a, at), piece(a, at), x_ssem.at[a, e], x_rsem.at[a, e],
            at_clus(zpos, 1 - xpos, core), coef,
        )

    def c_copy(a, f, e):
        at = at_clus(ring_z(e), xpos if f == 0 else 1 - xpos, core)
        return remote(
            piece(a, at), piece(a, at), c_ssem.at[a, f, e], c_rsem.at[a, f, e],
            at_clus(zpos, xpos, 1 - core), coef,
        )

    def rs_copy(a, d):
        to = at_coef(d)
        return remote(
            rs_send.at[a, to], rs_recv.at[a, d], rs_ssem.at[a, d], rs_rsem.at[a, d], clus, to,
        )

    def cp_copy(a, d):
        return remote(
            cp_send.at[a], cp_recv.at[a, d], cp_ssem.at[a, d], cp_rsem.at[a, d], clus, at_coef(d),
        )

    order = [0, chunks - 1] + list(range(1, chunks - 1))

    def apply_operator(a, values, result):
        own = pltpu.make_async_copy(
            values, ext[a].at[pl.ds(NWIN, leaves), my_rows], own_sem.at[a]
        )
        own.start()
        for d in range(1, nk):
            y_copy(a, values, d, order[0]).start()
        for up in (False, True):
            halo_start(a, values, 0, up)

        if a == 0:
            def combine(i, carry):
                grow[i // CHILD, pl.ds(pl.multiple_of(lax.rem(i, CHILD) * rows, rows), rows)] = jnp.dot(
                    basis[i], transfer[i], preferred_element_type=F32
                ).astype(BF16)
                return carry

            lax.fori_loop(0, leaves, combine, 0)

        parts = []
        for p in range(parents):
            mine = values[pl.ds(p * CHILD, CHILD)].reshape(CHILD * rows, vectors)
            part = lax.dot_general(
                grow[p], mine, (((0,), (0,)), ((), ())), preferred_element_type=F32
            )
            parts.append(part)
            for o in range(nk):
                rs_send[a, o, p] = part[o * share:(o + 1) * share].astype(BF16)
        for d in range(1, nk):
            rs_copy(a, d).start()
        for chunk in order[1:]:
            for d in range(1, nk):
                y_copy(a, values, d, chunk).start()

        if a == 0:
            for load in loads:
                load.wait()
            for p in range(parents):
                clhs[p] = jnp.concatenate([coupling[p, k] for k in range(far_k)], axis=1)

        total = rs_send[a, coef].astype(F32)
        for d in range(1, nk):
            rs_copy(a, d).wait_recv()
            total = total + rs_recv[a, d].astype(F32)
        pc[a][pl.ds(clus * parents, parents)] = total.astype(BF16)

        for e in range(1, outer):
            z_copy(a, e).start()
        x_copy(a, 0).start()
        c_copy(a, 0, 0).start()
        for e in range(1, outer):
            z_copy(a, outer - e).wait_recv()
            x_copy(a, e).start()
            c_copy(a, 0, e).start()
        for e in range(outer):
            x_copy(a, e).wait_recv()
            c_copy(a, 1, e).start()
        for f in range(2):
            for e in range(outer):
                c_copy(a, f, e).wait_recv()

        for up, chunk in ((False, 0), (True, chunks - 1)):
            for d in range(1, nk):
                y_copy(a, values, d, chunk).wait_recv()
                halo_start(a, values, d, up)

        for p in range(parents):
            picked = jnp.concatenate([pc[a][far_list[p, k]] for k in range(far_k)], axis=0)
            cp_send[a, p] = jnp.dot(clhs[p], picked, preferred_element_type=F32).astype(BF16)
        for d in range(1, nk):
            cp_copy(a, d).start()
        coupled = cp_send[a].astype(F32)
        for d in range(1, nk):
            cp_copy(a, d).wait_recv()
            coupled = coupled + cp_recv[a, d].astype(F32)
        coupled = coupled.astype(BF16)
        for p in range(parents):
            far[pl.ds(p * CHILD, CHILD)] = jnp.dot(
                grow[p], coupled[p], preferred_element_type=F32
            ).reshape(CHILD, rows, vectors)

        own.wait()
        for chunk in order[2:]:
            for d in range(1, nk):
                y_copy(a, values, d, chunk).wait_recv()
        for up in (False, True):
            for d in range(nk):
                halo_wait_recv(a, values, d, up)

        offset = clus * leaves - NWIN

        def near(i, carry):
            lhs = jnp.concatenate([nb[i, k] for k in range(near_k)], axis=1)
            rhs = jnp.concatenate(
                [ext[a][jnp.clip(near_list[i, k] - offset, 0, leaves + 2 * NWIN - 1)] for k in range(near_k)], axis=0
            )
            result[i] = (far[i] + jnp.dot(lhs, rhs, preferred_element_type=F32)).astype(BF16)
            return carry

        lax.fori_loop(0, leaves, near, 0)

    apply_operator(0, density, first)
    apply_operator(1, first, second)

    for a, values in ((0, density), (1, first)):
        for d in range(1, nk):
            rs_copy(a, d).wait_send()
            cp_copy(a, d).wait_send()
            for chunk in range(chunks):
                y_copy(a, values, d, chunk).wait_send()
        for up in (False, True):
            for d in range(nk):
                halo_wait_send(a, values, d, up)
        for e in range(1, outer):
            z_copy(a, e).wait_send()
        for e in range(outer):
            x_copy(a, e).wait_send()
            c_copy(a, 0, e).wait_send()
            c_copy(a, 1, e).wait_send()


def body(nc, nk, density, near_list, far_list, near_blocks, basis, transfer, coupling):
    leaves, rows, vectors = density.shape
    parents = leaves // CHILD
    rank, share = coupling.shape[2:]
    far_k = coupling.shape[1]
    outer = nc // 4
    chunks = leaves // NWIN
    vmem = pl.BlockSpec(memory_space=pltpu.VMEM)
    smem = pl.BlockSpec(memory_space=pltpu.SMEM)
    anywhere = pl.BlockSpec(memory_space=pl.ANY)
    dma = pltpu.SemaphoreType.DMA
    return pl.pallas_call(
        functools.partial(kernel, nc, nk),
        out_shape=(jax.ShapeDtypeStruct(density.shape, BF16),) * 2,
        in_specs=[vmem, smem, smem, anywhere, vmem, vmem, anywhere],
        out_specs=(vmem, vmem),
        scratch_shapes=[
            pltpu.VMEM(near_blocks.shape, BF16),
            pltpu.VMEM(coupling.shape, BF16),
            pltpu.VMEM((parents, rank, far_k * share), BF16),
            pltpu.VMEM((parents, CHILD * rows, rank), BF16),
            pltpu.VMEM((leaves + 2 * NWIN, rows * nk, vectors), BF16),
            pltpu.VMEM((leaves + 2 * NWIN, rows * nk, vectors), BF16),
            pltpu.VMEM((2, nk, parents, share, vectors), BF16),
            pltpu.VMEM((2, nk, parents, share, vectors), BF16),
            pltpu.VMEM((nc * parents, share, vectors), BF16),
            pltpu.VMEM((nc * parents, share, vectors), BF16),
            pltpu.VMEM((2, parents, rank, vectors), BF16),
            pltpu.VMEM((2, nk, parents, rank, vectors), BF16),
            pltpu.VMEM((leaves, rows, vectors), F32),
            dma((2,)),
            dma((2,)),
            dma((2, nk, chunks)),
            dma((2, nk, chunks)),
            dma((2, 2, nk)),
            dma((2, 2, nk)),
            dma((2, nk)),
            dma((2, nk)),
            dma((2, outer)),
            dma((2, outer)),
            dma((2, outer)),
            dma((2, outer)),
            dma((2, 2, outer)),
            dma((2, 2, outer)),
            dma((2, nk)),
            dma((2, nk)),
        ],
        compiler_params=pltpu.CompilerParams(
            collective_id=0, has_side_effects=True, vmem_limit_bytes=40 * 1024 * 1024
        ),
        cost_estimate=pl.CostEstimate(
            flops=4 * near_blocks.size * vectors, bytes_accessed=2 * near_blocks.size,
            transcendentals=0,
        ),
    )(density, near_list, far_list, near_blocks, basis, transfer, coupling)


def solution(mesh):
    placed = (
        P("clus", "coef", None),
        P("clus", None),
        P("clus", None),
        P("clus", None, "coef", None),
        P("clus", "coef", None),
        P("clus", None, None),
        P("clus", None, None, "coef"),
    )
    return jax.shard_map(
        functools.partial(body, mesh.shape["clus"], mesh.shape["coef"]),
        mesh=mesh,
        in_specs=placed,
        out_specs=(P("clus", "coef", None), P("clus", "coef", None)),
        check_vma=False,
    )
```

```python
import functools

import jax
import jax.numpy as jnp
from jax import lax
from jax.experimental import pallas as pl
from jax.experimental.pallas import tpu as pltpu
from jax.sharding import PartitionSpec as P

CHILD = 8
NWIN = 4
MESH = pl.DeviceIdType.MESH
F32 = jnp.float32
BF16 = jnp.bfloat16


def kernel(
    nc, nk,
    density_hbm, near_hbm, far_hbm, nb_hbm, basis_hbm, transfer_hbm, coupling_hbm,
    first, second,
    density, near_list, far_list, nb, basis, transfer, coupling,
    clhs, grow, ext_a, ext_b, window, rs_send, rs_recv, pc_a, pc_b, cp_send, cp_recv, acc,
    load_sem, own_sem, y_send, y_recv, h_send, h_recv, rs_ssem, rs_rsem,
    z_ssem, z_rsem, x_ssem, x_rsem, c_ssem, c_rsem, cp_ssem, cp_rsem,
):
    leaves, rows, vectors = density.shape
    parents = leaves // CHILD
    near_k = nb.shape[1]
    far_k = coupling.shape[1]
    share = coupling.shape[2]
    rank = grow.shape[2]
    outer = nc // 4
    chunks = leaves // NWIN
    clus = lax.axis_index("clus")
    coef = lax.axis_index("coef")
    core = lax.rem(clus, 2)
    xpos = lax.rem(clus // 2, 2)
    zpos = clus // 4
    ext = (ext_a, ext_b)
    pc = (pc_a, pc_b)
    my_rows = pl.ds(pl.multiple_of(coef * rows, rows), rows)

    loads = [
        pltpu.make_async_copy(src, dst, load_sem.at[n])
        for n, (src, dst) in enumerate((
            (density_hbm, density), (basis_hbm, basis), (transfer_hbm, transfer),
            (coupling_hbm, coupling), (far_hbm, far_list), (near_hbm, near_list), (nb_hbm, nb),
        ))
    ]
    for load in loads:
        load.start()

    def at_coef(d):
        return lax.rem(coef + d, nk)

    def at_clus(z, x, c):
        return (z * 2 + x) * 2 + c

    def ring_z(e):
        return lax.rem(zpos + e, outer)

    barrier = pltpu.get_barrier_semaphore()

    def greet(c, k):
        pl.semaphore_signal(barrier, inc=1, device_id=(c, k), device_id_type=MESH)

    for d in range(1, nk):
        greet(clus, at_coef(d))
    for e in range(1, outer):
        greet(at_clus(ring_z(e), xpos, core), coef)
    greet(at_clus(zpos, 1 - xpos, core), coef)
    greet(at_clus(zpos, xpos, 1 - core), coef)

    @pl.when(clus > 0)
    def _():
        greet(clus - 1, coef)

    @pl.when(clus < nc - 1)
    def _():
        greet(clus + 1, coef)

    pl.semaphore_wait(
        barrier, nk + outer + jnp.minimum(clus, 1) + jnp.minimum(nc - 1 - clus, 1)
    )

    def remote(src, dst, ssem, rsem, c, k):
        return pltpu.make_async_remote_copy(
            src_ref=src, dst_ref=dst, send_sem=ssem, recv_sem=rsem,
            device_id=(c, k), device_id_type=MESH,
        )

    def y_copy(a, values, d, chunk):
        start = chunk * NWIN
        return remote(
            values.at[pl.ds(start, NWIN)],
            ext[a].at[pl.ds(NWIN + start, NWIN), my_rows],
            y_send.at[a, d, chunk], y_recv.at[a, d, chunk], clus, at_coef(d),
        )

    def halo_copy(a, values, d, up):
        lo = leaves - NWIN if up else 0
        dst_lo = 0 if up else NWIN + leaves
        owner = lax.rem(coef + nk - d, nk)
        span = pl.ds(pl.multiple_of(owner * rows, rows), rows)
        src = values.at[pl.ds(lo, NWIN)] if d == 0 else ext[a].at[pl.ds(NWIN + lo, NWIN), span]
        side = 1 if up else 0
        return remote(
            src, ext[a].at[pl.ds(dst_lo, NWIN), span],
            h_send.at[a, side, d], h_recv.at[a, side, d], clus + (1 if up else -1), coef,
        )

    def halo_start(a, values, d, up):
        @pl.when((clus < nc - 1) if up else (clus > 0))
        def _():
            halo_copy(a, values, d, up).start()

    def halo_wait_send(a, values, d, up):
        @pl.when((clus < nc - 1) if up else (clus > 0))
        def _():
            halo_copy(a, values, d, up).wait_send()

    def halo_wait_recv(a, values, d, up):
        @pl.when((clus > 0) if up else (clus < nc - 1))
        def _():
            halo_copy(a, values, d, up).wait_recv()

    def piece(a, c):
        return pc[a].at[pl.ds(c * parents, parents)]

    def z_copy(a, e):
        return remote(
            piece(a, clus), piece(a, clus), z_ssem.at[a, e], z_rsem.at[a, e],
            at_clus(ring_z(e), xpos, core), coef,
        )

    def x_copy(a, e):
        at = at_clus(ring_z(e), xpos, core)
        return remote(
            piece(a, at), piece(a, at), x_ssem.at[a, e], x_rsem.at[a, e],
            at_clus(zpos, 1 - xpos, core), coef,
        )

    def c_copy(a, f, e):
        at = at_clus(ring_z(e), xpos if f == 0 else 1 - xpos, core)
        return remote(
            piece(a, at), piece(a, at), c_ssem.at[a, f, e], c_rsem.at[a, f, e],
            at_clus(zpos, xpos, 1 - core), coef,
        )

    def rs_copy(a, d):
        to = at_coef(d)
        return remote(
            rs_send.at[a, to], rs_recv.at[a, d], rs_ssem.at[a, d], rs_rsem.at[a, d], clus, to,
        )

    def cp_copy(a, d):
        return remote(
            cp_send.at[a], cp_recv.at[a, d], cp_ssem.at[a, d], cp_rsem.at[a, d], clus, at_coef(d),
        )

    order = [0, chunks - 1] + list(range(1, chunks - 1))
    offset = clus * leaves - NWIN

    def own_copy(a, values):
        return pltpu.make_async_copy(
            values, ext[a].at[pl.ds(NWIN, leaves), my_rows], own_sem.at[a]
        )

    def y_start(a, values, chunk):
        for d in range(1, nk):
            y_copy(a, values, d, chunk).start()

    def y_wait(a, values, chunk):
        for d in range(1, nk):
            y_copy(a, values, d, chunk).wait_recv()

    def near_sum(source, lo, start, count):
        last = source.shape[0] - 1

        def leaf(i, carry):
            lhs = jnp.concatenate([nb[i, k] for k in range(near_k)], axis=1)
            rhs = jnp.concatenate(
                [
                    source[jnp.clip(near_list[i, k] - offset - lo, 0, last)]
                    for k in range(near_k)
                ],
                axis=0,
            )
            acc[i] = jnp.dot(lhs, rhs, preferred_element_type=F32)
            return carry

        lax.fori_loop(start, start + count, leaf, 0)

    def lift(a, values):
        for p in range(parents):
            mine = values[pl.ds(p * CHILD, CHILD)].reshape(CHILD * rows, vectors)
            part = lax.dot_general(
                grow[p], mine, (((0,), (0,)), ((), ())), preferred_element_type=F32
            )
            for o in range(nk):
                rs_send[a, o, p] = part[o * share:(o + 1) * share].astype(BF16)
        for d in range(1, nk):
            rs_copy(a, d).start()

    def middle(a, values):
        total = rs_send[a, coef].astype(F32)
        for d in range(1, nk):
            rs_copy(a, d).wait_recv()
            total = total + rs_recv[a, d].astype(F32)
        pc[a][pl.ds(clus * parents, parents)] = total.astype(BF16)
        for e in range(1, outer):
            z_copy(a, e).start()
        x_copy(a, 0).start()
        c_copy(a, 0, 0).start()

        y_wait(a, values, 0)
        for d in range(1, nk):
            halo_start(a, values, d, False)

        for e in range(1, outer):
            z_copy(a, outer - e).wait_recv()
            x_copy(a, e).start()
            c_copy(a, 0, e).start()

        y_wait(a, values, chunks - 1)
        for d in range(1, nk):
            halo_start(a, values, d, True)

        for e in range(outer):
            x_copy(a, e).wait_recv()
            c_copy(a, 1, e).start()

        own_copy(a, values).wait()
        y_wait(a, values, 1)
        for d in range(nk):
            halo_wait_recv(a, values, d, True)
        window[...] = ext[a][pl.ds(0, 3 * NWIN)]
        near_sum(window, 0, 0, NWIN)

        for f in range(2):
            for e in range(outer):
                c_copy(a, f, e).wait_recv()
        for p in range(parents):
            picked = jnp.concatenate([pc[a][far_list[p, k]] for k in range(far_k)], axis=0)
            cp_send[a, p] = jnp.dot(clhs[p], picked, preferred_element_type=F32).astype(BF16)
        for d in range(1, nk):
            cp_copy(a, d).start()

        for chunk in range(2, chunks - 1):
            y_wait(a, values, chunk)
        for d in range(nk):
            halo_wait_recv(a, values, d, False)
        near_sum(ext[a], 0, NWIN, leaves - NWIN)

        coupled = cp_send[a].astype(F32)
        for d in range(1, nk):
            cp_copy(a, d).wait_recv()
            coupled = coupled + cp_recv[a, d].astype(F32)
        return coupled.astype(BF16)

    def finish(coupled, result, p):
        far = jnp.dot(grow[p], coupled[p], preferred_element_type=F32)
        span = pl.ds(p * CHILD, CHILD)
        result[span] = (acc[span] + far.reshape(CHILD, rows, vectors)).astype(BF16)

    loads[0].wait()
    own_copy(0, density).start()
    y_start(0, density, order[0])
    for up in (False, True):
        halo_start(0, density, 0, up)
    for n in (1, 2):
        loads[n].wait()

    def combine(i, carry):
        grow[i // CHILD, pl.ds(pl.multiple_of(lax.rem(i, CHILD) * rows, rows), rows)] = jnp.dot(
            basis[i], transfer[i], preferred_element_type=F32
        ).astype(BF16)
        return carry

    lax.fori_loop(0, leaves, combine, 0)
    lift(0, density)
    for chunk in order[1:]:
        y_start(0, density, chunk)
    for load in loads[3:]:
        load.wait()
    for p in range(parents):
        clhs[p] = coupling[p].reshape(far_k * share, rank).T

    coupled = middle(0, density)
    for p in range(parents):
        finish(coupled, first, p)
        if p == 0:
            y_start(1, first, order[0])
    lift(1, first)
    for up in (False, True):
        halo_start(1, first, 0, up)
    for chunk in order[1:]:
        y_start(1, first, chunk)
    own_copy(1, first).start()

    coupled = middle(1, first)
    for p in range(parents):
        finish(coupled, second, p)

    for a, values in ((0, density), (1, first)):
        for d in range(1, nk):
            rs_copy(a, d).wait_send()
            cp_copy(a, d).wait_send()
            for chunk in range(chunks):
                y_copy(a, values, d, chunk).wait_send()
        for up in (False, True):
            for d in range(nk):
                halo_wait_send(a, values, d, up)
        for e in range(1, outer):
            z_copy(a, e).wait_send()
        for e in range(outer):
            x_copy(a, e).wait_send()
            c_copy(a, 0, e).wait_send()
            c_copy(a, 1, e).wait_send()


def body(nc, nk, density, near_list, far_list, near_blocks, basis, transfer, coupling):
    coupling = jnp.swapaxes(coupling, 2, 3)
    leaves, rows, vectors = density.shape
    parents = leaves // CHILD
    share, rank = coupling.shape[2:]
    far_k = coupling.shape[1]
    outer = nc // 4
    chunks = leaves // NWIN
    vmem = pl.BlockSpec(memory_space=pltpu.VMEM)
    anywhere = pl.BlockSpec(memory_space=pl.ANY)
    dma = pltpu.SemaphoreType.DMA
    return pl.pallas_call(
        functools.partial(kernel, nc, nk),
        out_shape=(jax.ShapeDtypeStruct(density.shape, BF16),) * 2,
        in_specs=[anywhere] * 7,
        out_specs=(vmem, vmem),
        scratch_shapes=[
            pltpu.VMEM(density.shape, BF16),
            pltpu.SMEM(near_list.shape, jnp.int32),
            pltpu.SMEM(far_list.shape, jnp.int32),
            pltpu.VMEM(near_blocks.shape, BF16),
            pltpu.VMEM(basis.shape, BF16),
            pltpu.VMEM(transfer.shape, BF16),
            pltpu.VMEM(coupling.shape, BF16),
            pltpu.VMEM((parents, rank, far_k * share), BF16),
            pltpu.VMEM((parents, CHILD * rows, rank), BF16),
            pltpu.VMEM((leaves + 2 * NWIN, rows * nk, vectors), BF16),
            pltpu.VMEM((leaves + 2 * NWIN, rows * nk, vectors), BF16),
            pltpu.VMEM((3 * NWIN, rows * nk, vectors), BF16),
            pltpu.VMEM((2, nk, parents, share, vectors), BF16),
            pltpu.VMEM((2, nk, parents, share, vectors), BF16),
            pltpu.VMEM((nc * parents, share, vectors), BF16),
            pltpu.VMEM((nc * parents, share, vectors), BF16),
            pltpu.VMEM((2, parents, rank, vectors), BF16),
            pltpu.VMEM((2, nk, parents, rank, vectors), BF16),
            pltpu.VMEM((leaves, rows, vectors), F32),
            dma((7,)),
            dma((2,)),
            dma((2, nk, chunks)),
            dma((2, nk, chunks)),
            dma((2, 2, nk)),
            dma((2, 2, nk)),
            dma((2, nk)),
            dma((2, nk)),
            dma((2, outer)),
            dma((2, outer)),
            dma((2, outer)),
            dma((2, outer)),
            dma((2, 2, outer)),
            dma((2, 2, outer)),
            dma((2, nk)),
            dma((2, nk)),
        ],
        compiler_params=pltpu.CompilerParams(
            collective_id=0, has_side_effects=True, vmem_limit_bytes=56 * 1024 * 1024
        ),
        cost_estimate=pl.CostEstimate(
            flops=4 * near_blocks.size * vectors, bytes_accessed=2 * near_blocks.size,
            transcendentals=0,
        ),
    )(density, near_list, far_list, near_blocks, basis, transfer, coupling)


def solution(mesh):
    placed = (
        P("clus", "coef", None),
        P("clus", None),
        P("clus", None),
        P("clus", None, "coef", None),
        P("clus", "coef", None),
        P("clus", None, None),
        P("clus", None, None, "coef"),
    )
    return jax.shard_map(
        functools.partial(body, mesh.shape["clus"], mesh.shape["coef"]),
        mesh=mesh,
        in_specs=placed,
        out_specs=(P("clus", "coef", None), P("clus", "coef", None)),
        check_vma=False,
    )
```

```python
import functools

import jax
import jax.numpy as jnp
from jax import lax
from jax.experimental import pallas as pl
from jax.experimental.pallas import tpu as pltpu
from jax.sharding import PartitionSpec as P

CHILD = 8
NWIN = 4
MESH = pl.DeviceIdType.MESH
F32 = jnp.float32
BF16 = jnp.bfloat16


def kernel(
    nc, nk,
    density_hbm, near_hbm, far_hbm, nb_hbm, basis_hbm, transfer_hbm, coupling_hbm,
    first, second,
    density, near_list, far_list, nb, basis, transfer, coupling,
    clhs, grow, ext_a, ext_b, band, rs_send, rs_recv, pc_a, pc_b, cp_send, cp_recv, acc,
    load_sem, own_sem, y_send, y_recv, h_send, h_recv, rs_ssem, rs_rsem,
    z_ssem, z_rsem, x_ssem, x_rsem, c_ssem, c_rsem, cp_ssem, cp_rsem,
):
    leaves, rows, vectors = density.shape
    parents = leaves // CHILD
    near_k = nb.shape[1]
    far_k = coupling.shape[1]
    share = coupling.shape[2]
    rank = grow.shape[2]
    outer = nc // 4
    chunks = leaves // NWIN
    clus = lax.axis_index("clus")
    coef = lax.axis_index("coef")
    core = lax.rem(clus, 2)
    xpos = lax.rem(clus // 2, 2)
    zpos = clus // 4
    ext = (ext_a, ext_b)
    pc = (pc_a, pc_b)
    my_rows = pl.ds(pl.multiple_of(coef * rows, rows), rows)

    loads = [
        pltpu.make_async_copy(src, dst, load_sem.at[n])
        for n, (src, dst) in enumerate((
            (density_hbm, density), (basis_hbm, basis), (transfer_hbm, transfer),
            (coupling_hbm, coupling), (far_hbm, far_list), (near_hbm, near_list), (nb_hbm, nb),
        ))
    ]
    for load in loads:
        load.start()

    def at_coef(d):
        return lax.rem(coef + d, nk)

    def at_clus(z, x, c):
        return (z * 2 + x) * 2 + c

    def ring_z(e):
        return lax.rem(zpos + e, outer)

    barrier = pltpu.get_barrier_semaphore()

    def greet(c, k):
        pl.semaphore_signal(barrier, inc=1, device_id=(c, k), device_id_type=MESH)

    for d in range(1, nk):
        greet(clus, at_coef(d))
    for e in range(1, outer):
        greet(at_clus(ring_z(e), xpos, core), coef)
    greet(at_clus(zpos, 1 - xpos, core), coef)
    greet(at_clus(zpos, xpos, 1 - core), coef)

    @pl.when(clus > 0)
    def _():
        greet(clus - 1, coef)

    @pl.when(clus < nc - 1)
    def _():
        greet(clus + 1, coef)

    pl.semaphore_wait(
        barrier, nk + outer + jnp.minimum(clus, 1) + jnp.minimum(nc - 1 - clus, 1)
    )

    def remote(src, dst, ssem, rsem, c, k):
        return pltpu.make_async_remote_copy(
            src_ref=src, dst_ref=dst, send_sem=ssem, recv_sem=rsem,
            device_id=(c, k), device_id_type=MESH,
        )

    def y_copy(a, values, d, chunk):
        start = chunk * NWIN
        return remote(
            values.at[pl.ds(start, NWIN)],
            ext[a].at[pl.ds(NWIN + start, NWIN), my_rows],
            y_send.at[a, d, chunk], y_recv.at[a, d, chunk], clus, at_coef(d),
        )

    def halo_copy(a, values, d, up):
        lo = leaves - NWIN if up else 0
        dst_lo = 0 if up else NWIN + leaves
        owner = lax.rem(coef + nk - d, nk)
        span = pl.ds(pl.multiple_of(owner * rows, rows), rows)
        src = values.at[pl.ds(lo, NWIN)] if d == 0 else ext[a].at[pl.ds(NWIN + lo, NWIN), span]
        side = 1 if up else 0
        return remote(
            src, ext[a].at[pl.ds(dst_lo, NWIN), span],
            h_send.at[a, side, d], h_recv.at[a, side, d], clus + (1 if up else -1), coef,
        )

    def halo_start(a, values, d, up):
        @pl.when((clus < nc - 1) if up else (clus > 0))
        def _():
            halo_copy(a, values, d, up).start()

    def halo_wait_send(a, values, d, up):
        @pl.when((clus < nc - 1) if up else (clus > 0))
        def _():
            halo_copy(a, values, d, up).wait_send()

    def halo_wait_recv(a, values, d, up):
        @pl.when((clus > 0) if up else (clus < nc - 1))
        def _():
            halo_copy(a, values, d, up).wait_recv()

    def piece(a, c):
        return pc[a].at[pl.ds(c * parents, parents)]

    def z_copy(a, e):
        return remote(
            piece(a, clus), piece(a, clus), z_ssem.at[a, e], z_rsem.at[a, e],
            at_clus(ring_z(e), xpos, core), coef,
        )

    def x_copy(a, e):
        at = at_clus(ring_z(e), xpos, core)
        return remote(
            piece(a, at), piece(a, at), x_ssem.at[a, e], x_rsem.at[a, e],
            at_clus(zpos, 1 - xpos, core), coef,
        )

    def c_copy(a, f, e):
        at = at_clus(ring_z(e), xpos if f == 0 else 1 - xpos, core)
        return remote(
            piece(a, at), piece(a, at), c_ssem.at[a, f, e], c_rsem.at[a, f, e],
            at_clus(zpos, xpos, 1 - core), coef,
        )

    def rs_copy(a, d):
        to = at_coef(d)
        return remote(
            rs_send.at[a, to], rs_recv.at[a, d], rs_ssem.at[a, d], rs_rsem.at[a, d], clus, to,
        )

    def cp_copy(a, d):
        return remote(
            cp_send.at[a], cp_recv.at[a, d], cp_ssem.at[a, d], cp_rsem.at[a, d], clus, at_coef(d),
        )

    order = [0, chunks - 1] + list(range(1, chunks - 1))
    offset = clus * leaves - NWIN

    def own_copy(a, values):
        return pltpu.make_async_copy(
            values, ext[a].at[pl.ds(NWIN, leaves), my_rows], own_sem.at[a]
        )

    def y_start(a, values, chunk):
        for d in range(1, nk):
            y_copy(a, values, d, chunk).start()

    def y_wait(a, values, chunk):
        for d in range(1, nk):
            y_copy(a, values, d, chunk).wait_recv()

    def build_band():
        def leaf(i, carry):
            t, at = i // NWIN, lax.rem(i, NWIN)
            span = pl.ds(pl.multiple_of(at * rows, rows), rows)
            for o in range(2 * NWIN + 1):
                total = jnp.zeros((rows, nb.shape[3]), BF16)
                for k in range(near_k):
                    same = near_list[i, k] == offset + i + o
                    total = total + jnp.where(same, nb[i, k], jnp.zeros_like(total))
                band[t, at + o, span] = total
            for o in range(2 * NWIN + 1, 3 * NWIN):
                band[t, lax.rem(at + o, 3 * NWIN), span] = jnp.zeros((rows, nb.shape[3]), BF16)
            return carry

        lax.fori_loop(0, leaves, leaf, 0)

    def near_from(a, s, seen):
        panel_rows = rows * nk
        source = ext[a][pl.ds((s + 1) * NWIN, NWIN)].reshape(NWIN * panel_rows, vectors)
        for t in (s - 1, s, s + 1):
            if 0 <= t < chunks:
                first_slot = (s - t + 1) * NWIN
                lhs = jnp.concatenate(
                    [band[t, first_slot + n] for n in range(NWIN)], axis=1
                )
                part = jnp.dot(lhs, source, preferred_element_type=F32)
                acc[t] = acc[t] + part if t in seen else part
                seen.add(t)

    def lift(a, values):
        for p in range(parents):
            mine = values[pl.ds(p * CHILD, CHILD)].reshape(CHILD * rows, vectors)
            part = lax.dot_general(
                grow[p], mine, (((0,), (0,)), ((), ())), preferred_element_type=F32
            )
            for o in range(nk):
                rs_send[a, o, p] = part[o * share:(o + 1) * share].astype(BF16)
        for d in range(1, nk):
            rs_copy(a, d).start()

    def middle(a, values):
        total = rs_send[a, coef].astype(F32)
        for d in range(1, nk):
            rs_copy(a, d).wait_recv()
            total = total + rs_recv[a, d].astype(F32)
        pc[a][pl.ds(clus * parents, parents)] = total.astype(BF16)
        for e in range(1, outer):
            z_copy(a, e).start()
        x_copy(a, 0).start()
        c_copy(a, 0, 0).start()

        if a == 0:
            for load in loads[3:]:
                load.wait()
            for p in range(parents):
                clhs[p] = coupling[p].reshape(far_k * share, rank).T
            build_band()

        for e in range(1, outer):
            z_copy(a, outer - e).wait_recv()
            x_copy(a, e).start()
            c_copy(a, 0, e).start()

        seen = set()
        y_wait(a, values, 0)
        for d in range(1, nk):
            halo_start(a, values, d, False)
        own_copy(a, values).wait()
        near_from(a, 0, seen)
        y_wait(a, values, chunks - 1)
        for d in range(1, nk):
            halo_start(a, values, d, True)
        near_from(a, chunks - 1, seen)

        for e in range(outer):
            x_copy(a, e).wait_recv()
            c_copy(a, 1, e).start()
        for s in range(1, chunks - 2):
            y_wait(a, values, s)
            near_from(a, s, seen)

        for f in range(2):
            for e in range(outer):
                c_copy(a, f, e).wait_recv()
        for p in range(parents):
            picked = jnp.concatenate([pc[a][far_list[p, k]] for k in range(far_k)], axis=0)
            cp_send[a, p] = jnp.dot(clhs[p], picked, preferred_element_type=F32).astype(BF16)
        for d in range(1, nk):
            cp_copy(a, d).start()

        for up, s in ((True, -1), (False, chunks)):
            for d in range(nk):
                halo_wait_recv(a, values, d, up)
            near_from(a, s, seen)
        y_wait(a, values, chunks - 2)
        near_from(a, chunks - 2, seen)

        coupled = cp_send[a].astype(F32)
        for d in range(1, nk):
            cp_copy(a, d).wait_recv()
            coupled = coupled + cp_recv[a, d].astype(F32)
        return coupled.astype(BF16)

    def finish(coupled, result, p):
        far = jnp.dot(grow[p], coupled[p], preferred_element_type=F32)
        span = pl.ds(p * CHILD, CHILD)
        near = acc[pl.ds(p * (CHILD // NWIN), CHILD // NWIN)].reshape(CHILD, rows, vectors)
        result[span] = (near + far.reshape(CHILD, rows, vectors)).astype(BF16)

    loads[0].wait()
    own_copy(0, density).start()
    y_start(0, density, order[0])
    for up in (False, True):
        halo_start(0, density, 0, up)
    for n in (1, 2):
        loads[n].wait()

    for i in range(leaves):
        grow[i // CHILD, pl.ds(i % CHILD * rows, rows)] = jnp.dot(
            basis[i], transfer[i], preferred_element_type=F32
        ).astype(BF16)
    lift(0, density)
    for chunk in order[1:]:
        y_start(0, density, chunk)

    @pl.when(clus == 0)
    def _():
        for buffer in ext:
            buffer[pl.ds(0, NWIN)] = jnp.zeros((NWIN,) + buffer.shape[1:], BF16)

    @pl.when(clus == nc - 1)
    def _():
        for buffer in ext:
            buffer[pl.ds(NWIN + leaves, NWIN)] = jnp.zeros((NWIN,) + buffer.shape[1:], BF16)

    coupled = middle(0, density)
    for p in range(parents):
        finish(coupled, first, p)
        if p == 0:
            y_start(1, first, order[0])
    lift(1, first)
    for up in (False, True):
        halo_start(1, first, 0, up)
    for chunk in order[1:]:
        y_start(1, first, chunk)
    own_copy(1, first).start()

    coupled = middle(1, first)
    for p in range(parents):
        finish(coupled, second, p)

    for a, values in ((0, density), (1, first)):
        for d in range(1, nk):
            rs_copy(a, d).wait_send()
            cp_copy(a, d).wait_send()
            for chunk in range(chunks):
                y_copy(a, values, d, chunk).wait_send()
        for up in (False, True):
            for d in range(nk):
                halo_wait_send(a, values, d, up)
        for e in range(1, outer):
            z_copy(a, e).wait_send()
        for e in range(outer):
            x_copy(a, e).wait_send()
            c_copy(a, 0, e).wait_send()
            c_copy(a, 1, e).wait_send()


def hand_over(pieces, first, second, first_out, second_out, sem):
    size = first.shape[0] // pieces
    copies = [
        pltpu.make_async_copy(
            src.at[pl.ds(n * size, size)], dst.at[pl.ds(n * size, size)], sem.at[m, n]
        )
        for m, (src, dst) in enumerate(((first, first_out), (second, second_out)))
        for n in range(pieces)
    ]
    for copy in copies:
        copy.start()
    for copy in copies:
        copy.wait()


def body(nc, nk, density, near_list, far_list, near_blocks, basis, transfer, coupling):
    coupling = jnp.swapaxes(coupling, 2, 3)
    leaves, rows, vectors = density.shape
    parents = leaves // CHILD
    share, rank = coupling.shape[2:]
    far_k = coupling.shape[1]
    outer = nc // 4
    chunks = leaves // NWIN
    vmem = pl.BlockSpec(memory_space=pltpu.VMEM)
    anywhere = pl.BlockSpec(memory_space=pl.ANY)
    dma = pltpu.SemaphoreType.DMA
    held = pl.pallas_call(
        functools.partial(kernel, nc, nk),
        out_shape=(jax.ShapeDtypeStruct(density.shape, BF16),) * 2,
        in_specs=[anywhere] * 7,
        out_specs=(vmem, vmem),
        scratch_shapes=[
            pltpu.VMEM(density.shape, BF16),
            pltpu.SMEM(near_list.shape, jnp.int32),
            pltpu.SMEM(far_list.shape, jnp.int32),
            pltpu.VMEM(near_blocks.shape, BF16),
            pltpu.VMEM(basis.shape, BF16),
            pltpu.VMEM(transfer.shape, BF16),
            pltpu.VMEM(coupling.shape, BF16),
            pltpu.VMEM((parents, rank, far_k * share), BF16),
            pltpu.VMEM((parents, CHILD * rows, rank), BF16),
            pltpu.VMEM((leaves + 2 * NWIN, rows * nk, vectors), BF16),
            pltpu.VMEM((leaves + 2 * NWIN, rows * nk, vectors), BF16),
            pltpu.VMEM((chunks, 3 * NWIN, NWIN * rows, near_blocks.shape[3]), BF16),
            pltpu.VMEM((2, nk, parents, share, vectors), BF16),
            pltpu.VMEM((2, nk, parents, share, vectors), BF16),
            pltpu.VMEM((nc * parents, share, vectors), BF16),
            pltpu.VMEM((nc * parents, share, vectors), BF16),
            pltpu.VMEM((2, parents, rank, vectors), BF16),
            pltpu.VMEM((2, nk, parents, rank, vectors), BF16),
            pltpu.VMEM((chunks, NWIN * rows, vectors), F32),
            dma((7,)),
            dma((2,)),
            dma((2, nk, chunks)),
            dma((2, nk, chunks)),
            dma((2, 2, nk)),
            dma((2, 2, nk)),
            dma((2, nk)),
            dma((2, nk)),
            dma((2, outer)),
            dma((2, outer)),
            dma((2, outer)),
            dma((2, outer)),
            dma((2, 2, outer)),
            dma((2, 2, outer)),
            dma((2, nk)),
            dma((2, nk)),
        ],
        compiler_params=pltpu.CompilerParams(
            collective_id=0, has_side_effects=True, vmem_limit_bytes=56 * 1024 * 1024
        ),
        cost_estimate=pl.CostEstimate(
            flops=4 * near_blocks.size * vectors, bytes_accessed=2 * near_blocks.size,
            transcendentals=0,
        ),
    )(density, near_list, far_list, near_blocks, basis, transfer, coupling)
    return pl.pallas_call(
        functools.partial(hand_over, chunks),
        out_shape=(jax.ShapeDtypeStruct(density.shape, BF16),) * 2,
        in_specs=[anywhere] * 2,
        out_specs=(anywhere,) * 2,
        scratch_shapes=[dma((2, chunks))],
        compiler_params=pltpu.CompilerParams(vmem_limit_bytes=56 * 1024 * 1024),
    )(*held)


def solution(mesh):
    placed = (
        P("clus", "coef", None),
        P("clus", None),
        P("clus", None),
        P("clus", None, "coef", None),
        P("clus", "coef", None),
        P("clus", None, None),
        P("clus", None, None, "coef"),
    )
    return jax.shard_map(
        functools.partial(body, mesh.shape["clus"], mesh.shape["coef"]),
        mesh=mesh,
        in_specs=placed,
        out_specs=(P("clus", "coef", None), P("clus", "coef", None)),
        check_vma=False,
    )
```

```python
import functools

import jax
import jax.numpy as jnp
from jax import lax
from jax.experimental import pallas as pl
from jax.experimental.pallas import tpu as pltpu
from jax.sharding import PartitionSpec as P

CHILD = 8
NWIN = 4
MESH = pl.DeviceIdType.MESH
F32 = jnp.float32
BF16 = jnp.bfloat16


def kernel(
    nc, nk,
    density_hbm, near_hbm, far_hbm, nb_hbm, basis_hbm, transfer_hbm, coupling_hbm,
    first, second,
    density, near_list, far_list, nb, basis, transfer, coupling,
    clhs, grow, ext_a, ext_b, band, rs_send, rs_recv, pc_a, pc_b, cp_send, cp_recv, acc,
    load_sem, y_send, y_recv, h_send, h_recv, rs_ssem, rs_rsem,
    z_ssem, z_rsem, x_ssem, x_rsem, c_ssem, c_rsem, cp_ssem, cp_rsem,
):
    leaves, rows, vectors = density.shape
    parents = leaves // CHILD
    near_k = nb.shape[1]
    far_k = coupling.shape[1]
    share = coupling.shape[2]
    rank = grow.shape[2]
    outer = nc // 4
    chunks = leaves // NWIN
    clus = lax.axis_index("clus")
    coef = lax.axis_index("coef")
    core = lax.rem(clus, 2)
    xpos = lax.rem(clus // 2, 2)
    zpos = clus // 4
    ext = (ext_a, ext_b)
    pc = (pc_a, pc_b)
    my_rows = pl.ds(pl.multiple_of(coef * rows, rows), rows)

    loads = [
        pltpu.make_async_copy(src, dst, load_sem.at[n])
        for n, (src, dst) in enumerate((
            (density_hbm, density), (basis_hbm, basis), (transfer_hbm, transfer),
            (coupling_hbm, coupling), (far_hbm, far_list), (near_hbm, near_list), (nb_hbm, nb),
        ))
    ]
    for load in loads:
        load.start()

    def at_coef(d):
        return lax.rem(coef + d, nk)

    def at_clus(z, x, c):
        return (z * 2 + x) * 2 + c

    def ring_z(e):
        return lax.rem(zpos + e, outer)

    barrier = pltpu.get_barrier_semaphore()

    def greet(c, k):
        pl.semaphore_signal(barrier, inc=1, device_id=(c, k), device_id_type=MESH)

    for d in range(1, nk):
        greet(clus, at_coef(d))
    for e in range(1, outer):
        greet(at_clus(ring_z(e), xpos, core), coef)
    greet(at_clus(zpos, 1 - xpos, core), coef)
    greet(at_clus(zpos, xpos, 1 - core), coef)

    @pl.when(clus > 0)
    def _():
        greet(clus - 1, coef)

    @pl.when(clus < nc - 1)
    def _():
        greet(clus + 1, coef)

    pl.semaphore_wait(
        barrier, nk + outer + jnp.minimum(clus, 1) + jnp.minimum(nc - 1 - clus, 1)
    )

    def remote(src, dst, ssem, rsem, c, k):
        return pltpu.make_async_remote_copy(
            src_ref=src, dst_ref=dst, send_sem=ssem, recv_sem=rsem,
            device_id=(c, k), device_id_type=MESH,
        )

    def y_copy(a, values, d, chunk):
        start = chunk * NWIN
        return remote(
            values.at[pl.ds(start, NWIN)],
            ext[a].at[pl.ds(NWIN + start, NWIN), my_rows],
            y_send.at[a, d, chunk], y_recv.at[a, d, chunk], clus, at_coef(d),
        )

    def halo_copy(a, values, d, up):
        lo = leaves - NWIN if up else 0
        dst_lo = 0 if up else NWIN + leaves
        owner = lax.rem(coef + nk - d, nk)
        span = pl.ds(pl.multiple_of(owner * rows, rows), rows)
        src = values.at[pl.ds(lo, NWIN)] if d == 0 else ext[a].at[pl.ds(NWIN + lo, NWIN), span]
        side = 1 if up else 0
        return remote(
            src, ext[a].at[pl.ds(dst_lo, NWIN), span],
            h_send.at[a, side, d], h_recv.at[a, side, d], clus + (1 if up else -1), coef,
        )

    def halo_start(a, values, d, up):
        @pl.when((clus < nc - 1) if up else (clus > 0))
        def _():
            halo_copy(a, values, d, up).start()

    def halo_wait_send(a, values, d, up):
        @pl.when((clus < nc - 1) if up else (clus > 0))
        def _():
            halo_copy(a, values, d, up).wait_send()

    def halo_wait_recv(a, values, d, up):
        @pl.when((clus > 0) if up else (clus < nc - 1))
        def _():
            halo_copy(a, values, d, up).wait_recv()

    def piece(a, c):
        return pc[a].at[pl.ds(c * parents, parents)]

    def z_copy(a, e):
        return remote(
            piece(a, clus), piece(a, clus), z_ssem.at[a, e], z_rsem.at[a, e],
            at_clus(ring_z(e), xpos, core), coef,
        )

    def x_copy(a, e):
        at = at_clus(ring_z(e), xpos, core)
        return remote(
            piece(a, at), piece(a, at), x_ssem.at[a, e], x_rsem.at[a, e],
            at_clus(zpos, 1 - xpos, core), coef,
        )

    def c_copy(a, f, e):
        at = at_clus(ring_z(e), xpos if f == 0 else 1 - xpos, core)
        return remote(
            piece(a, at), piece(a, at), c_ssem.at[a, f, e], c_rsem.at[a, f, e],
            at_clus(zpos, xpos, 1 - core), coef,
        )

    def rs_copy(a, d):
        to = at_coef(d)
        return remote(
            rs_send.at[a, to], rs_recv.at[a, d], rs_ssem.at[a, d], rs_rsem.at[a, d], clus, to,
        )

    def cp_copy(a, d):
        return remote(
            cp_send.at[a], cp_recv.at[a, d], cp_ssem.at[a, d], cp_rsem.at[a, d], clus, at_coef(d),
        )

    order = [0, chunks - 1] + list(range(1, chunks - 1))
    offset = clus * leaves - NWIN

    def keep_own(a, values, start, count):
        for i in range(start, start + count):
            ext[a][NWIN + i, my_rows] = values[i]

    def y_start(a, values, chunk):
        for d in range(1, nk):
            y_copy(a, values, d, chunk).start()

    def y_wait(a, values, chunk):
        for d in range(1, nk):
            y_copy(a, values, d, chunk).wait_recv()

    def build_band():
        def leaf(i, carry):
            t, at = i // NWIN, lax.rem(i, NWIN)
            span = pl.ds(pl.multiple_of(at * rows, rows), rows)
            for o in range(2 * NWIN + 1):
                total = jnp.zeros((rows, nb.shape[3]), BF16)
                for k in range(near_k):
                    same = near_list[i, k] == offset + i + o
                    total = total + jnp.where(same, nb[i, k], jnp.zeros_like(total))
                band[t, at + o, span] = total
            for o in range(2 * NWIN + 1, 3 * NWIN):
                band[t, lax.rem(at + o, 3 * NWIN), span] = jnp.zeros((rows, nb.shape[3]), BF16)
            return carry

        lax.fori_loop(0, leaves, leaf, 0)

    def near_from(a, s, seen):
        panel_rows = rows * nk
        source = ext[a][pl.ds((s + 1) * NWIN, NWIN)].reshape(NWIN * panel_rows, vectors)
        for t in (s - 1, s, s + 1):
            if 0 <= t < chunks:
                first_slot = (s - t + 1) * NWIN
                lhs = jnp.concatenate(
                    [band[t, first_slot + n] for n in range(NWIN)], axis=1
                )
                part = jnp.dot(lhs, source, preferred_element_type=F32)
                acc[t] = acc[t] + part if t in seen else part
                seen.add(t)

    def lift(a, values):
        for p in range(parents):
            mine = values[pl.ds(p * CHILD, CHILD)].reshape(CHILD * rows, vectors)
            part = lax.dot_general(
                grow[p], mine, (((0,), (0,)), ((), ())), preferred_element_type=F32
            )
            for o in range(nk):
                rs_send[a, o, p] = part[o * share:(o + 1) * share].astype(BF16)
        for d in range(1, nk):
            rs_copy(a, d).start()

    def middle(a, values):
        total = rs_send[a, coef].astype(F32)
        for d in range(1, nk):
            rs_copy(a, d).wait_recv()
            total = total + rs_recv[a, d].astype(F32)
        pc[a][pl.ds(clus * parents, parents)] = total.astype(BF16)
        for e in range(1, outer):
            z_copy(a, e).start()
        x_copy(a, 0).start()
        c_copy(a, 0, 0).start()

        if a == 0:
            for load in loads[3:]:
                load.wait()
            for p in range(parents):
                clhs[p] = coupling[p].reshape(far_k * share, rank).T
            build_band()

        for e in range(1, outer):
            z_copy(a, outer - e).wait_recv()
            x_copy(a, e).start()
            c_copy(a, 0, e).start()

        y_wait(a, values, 0)
        for d in range(1, nk):
            halo_start(a, values, d, False)
        for e in range(outer):
            x_copy(a, e).wait_recv()
            c_copy(a, 1, e).start()

        y_wait(a, values, chunks - 1)
        for d in range(1, nk):
            halo_start(a, values, d, True)
        seen = set()
        near_from(a, 0, seen)
        near_from(a, chunks - 1, seen)

        for f in range(2):
            for e in range(outer):
                c_copy(a, f, e).wait_recv()
        for p in range(parents):
            picked = jnp.concatenate([pc[a][far_list[p, k]] for k in range(far_k)], axis=0)
            cp_send[a, p] = jnp.dot(clhs[p], picked, preferred_element_type=F32).astype(BF16)
        for d in range(1, nk):
            cp_copy(a, d).start()

        for up, s in ((True, -1), (False, chunks)):
            for d in range(nk):
                halo_wait_recv(a, values, d, up)
            near_from(a, s, seen)
        for s in range(1, chunks - 1):
            y_wait(a, values, s)
            near_from(a, s, seen)

        coupled = cp_send[a].astype(F32)
        for d in range(1, nk):
            cp_copy(a, d).wait_recv()
            coupled = coupled + cp_recv[a, d].astype(F32)
        return coupled.astype(BF16)

    def finish(coupled, result, p):
        far = jnp.dot(grow[p], coupled[p], preferred_element_type=F32)
        span = pl.ds(p * CHILD, CHILD)
        near = acc[pl.ds(p * (CHILD // NWIN), CHILD // NWIN)].reshape(CHILD, rows, vectors)
        result[span] = (near + far.reshape(CHILD, rows, vectors)).astype(BF16)

    loads[0].wait()
    y_start(0, density, order[0])
    for up in (False, True):
        halo_start(0, density, 0, up)
    for n in (1, 2):
        loads[n].wait()

    for i in range(leaves):
        grow[i // CHILD, pl.ds(i % CHILD * rows, rows)] = jnp.dot(
            basis[i], transfer[i], preferred_element_type=F32
        ).astype(BF16)
    lift(0, density)
    for chunk in order[1:]:
        y_start(0, density, chunk)
    keep_own(0, density, 0, leaves)

    @pl.when(clus == 0)
    def _():
        for buffer in ext:
            buffer[pl.ds(0, NWIN)] = jnp.zeros((NWIN,) + buffer.shape[1:], BF16)

    @pl.when(clus == nc - 1)
    def _():
        for buffer in ext:
            buffer[pl.ds(NWIN + leaves, NWIN)] = jnp.zeros((NWIN,) + buffer.shape[1:], BF16)

    coupled = middle(0, density)
    for p in range(parents):
        finish(coupled, first, p)
        if p == 0:
            y_start(1, first, order[0])
    lift(1, first)
    for up in (False, True):
        halo_start(1, first, 0, up)
    for chunk in order[1:]:
        y_start(1, first, chunk)
    keep_own(1, first, 0, leaves)

    coupled = middle(1, first)
    for p in range(parents):
        finish(coupled, second, p)

    for a, values in ((0, density), (1, first)):
        for d in range(1, nk):
            rs_copy(a, d).wait_send()
            cp_copy(a, d).wait_send()
            for chunk in range(chunks):
                y_copy(a, values, d, chunk).wait_send()
        for up in (False, True):
            for d in range(nk):
                halo_wait_send(a, values, d, up)
        for e in range(1, outer):
            z_copy(a, e).wait_send()
        for e in range(outer):
            x_copy(a, e).wait_send()
            c_copy(a, 0, e).wait_send()
            c_copy(a, 1, e).wait_send()


def hand_over(first, second, first_out, second_out):
    first_out[...] = first[...]
    second_out[...] = second[...]


def body(nc, nk, density, near_list, far_list, near_blocks, basis, transfer, coupling):
    coupling = jnp.swapaxes(coupling, 2, 3)
    leaves, rows, vectors = density.shape
    parents = leaves // CHILD
    share, rank = coupling.shape[2:]
    far_k = coupling.shape[1]
    outer = nc // 4
    chunks = leaves // NWIN
    vmem = pl.BlockSpec(memory_space=pltpu.VMEM)
    anywhere = pl.BlockSpec(memory_space=pl.ANY)
    block = pl.BlockSpec((NWIN, rows, vectors), lambda n: (n, 0, 0))
    dma = pltpu.SemaphoreType.DMA
    held = pl.pallas_call(
        functools.partial(kernel, nc, nk),
        out_shape=(jax.ShapeDtypeStruct(density.shape, BF16),) * 2,
        in_specs=[anywhere] * 7,
        out_specs=(vmem, vmem),
        scratch_shapes=[
            pltpu.VMEM(density.shape, BF16),
            pltpu.SMEM(near_list.shape, jnp.int32),
            pltpu.SMEM(far_list.shape, jnp.int32),
            pltpu.VMEM(near_blocks.shape, BF16),
            pltpu.VMEM(basis.shape, BF16),
            pltpu.VMEM(transfer.shape, BF16),
            pltpu.VMEM(coupling.shape, BF16),
            pltpu.VMEM((parents, rank, far_k * share), BF16),
            pltpu.VMEM((parents, CHILD * rows, rank), BF16),
            pltpu.VMEM((leaves + 2 * NWIN, rows * nk, vectors), BF16),
            pltpu.VMEM((leaves + 2 * NWIN, rows * nk, vectors), BF16),
            pltpu.VMEM((chunks, 3 * NWIN, NWIN * rows, near_blocks.shape[3]), BF16),
            pltpu.VMEM((2, nk, parents, share, vectors), BF16),
            pltpu.VMEM((2, nk, parents, share, vectors), BF16),
            pltpu.VMEM((nc * parents, share, vectors), BF16),
            pltpu.VMEM((nc * parents, share, vectors), BF16),
            pltpu.VMEM((2, parents, rank, vectors), BF16),
            pltpu.VMEM((2, nk, parents, rank, vectors), BF16),
            pltpu.VMEM((chunks, NWIN * rows, vectors), F32),
            dma((7,)),
            dma((2, nk, chunks)),
            dma((2, nk, chunks)),
            dma((2, 2, nk)),
            dma((2, 2, nk)),
            dma((2, nk)),
            dma((2, nk)),
            dma((2, outer)),
            dma((2, outer)),
            dma((2, outer)),
            dma((2, outer)),
            dma((2, 2, outer)),
            dma((2, 2, outer)),
            dma((2, nk)),
            dma((2, nk)),
        ],
        compiler_params=pltpu.CompilerParams(
            collective_id=0, has_side_effects=True, vmem_limit_bytes=56 * 1024 * 1024
        ),
        cost_estimate=pl.CostEstimate(
            flops=4 * near_blocks.size * vectors, bytes_accessed=2 * near_blocks.size,
            transcendentals=0,
        ),
    )(density, near_list, far_list, near_blocks, basis, transfer, coupling)
    return pl.pallas_call(
        hand_over,
        out_shape=(jax.ShapeDtypeStruct(density.shape, BF16),) * 2,
        grid=(chunks,),
        in_specs=[block] * 2,
        out_specs=(block,) * 2,
        compiler_params=pltpu.CompilerParams(vmem_limit_bytes=56 * 1024 * 1024),
    )(*held)


def solution(mesh):
    placed = (
        P("clus", "coef", None),
        P("clus", None),
        P("clus", None),
        P("clus", None, "coef", None),
        P("clus", "coef", None),
        P("clus", None, None),
        P("clus", None, None, "coef"),
    )
    return jax.shard_map(
        functools.partial(body, mesh.shape["clus"], mesh.shape["coef"]),
        mesh=mesh,
        in_specs=placed,
        out_specs=(P("clus", "coef", None), P("clus", "coef", None)),
        check_vma=False,
    )
```

```python
import functools

import jax
import jax.numpy as jnp
from jax import lax
from jax.experimental import pallas as pl
from jax.experimental.pallas import tpu as pltpu
from jax.sharding import PartitionSpec as P

CHILD = 8
NWIN = 4
MESH = pl.DeviceIdType.MESH
F32 = jnp.float32
BF16 = jnp.bfloat16


def kernel(
    nc, nk,
    density_hbm, near_hbm, far_hbm, nb_hbm, basis_hbm, transfer_hbm, coupling_hbm,
    first, second,
    density, near_list, far_list, nb, basis, transfer, coupling,
    clhs, grow, grow_t, ext_a, ext_b, band, rs_send, rs_recv, pc_a, pc_b, cp_send, cp_recv, acc,
    load_sem, y_send, y_recv, h_send, h_recv, rs_ssem, rs_rsem,
    g_ssem, g_rsem, c_ssem, c_rsem, cp_ssem, cp_rsem,
):
    leaves, rows, vectors = density.shape
    parents = leaves // CHILD
    near_k = nb.shape[1]
    far_k = coupling.shape[1]
    share = coupling.shape[2]
    rank = grow.shape[2]
    outer = nc // 4
    chunks = leaves // NWIN
    clus = lax.axis_index("clus")
    coef = lax.axis_index("coef")
    core = lax.rem(clus, 2)
    xpos = lax.rem(clus // 2, 2)
    zpos = clus // 4
    ext = (ext_a, ext_b)
    pc = (pc_a, pc_b)
    my_rows = pl.ds(pl.multiple_of(coef * rows, rows), rows)

    loads = [
        pltpu.make_async_copy(src, dst, load_sem.at[n])
        for n, (src, dst) in enumerate((
            (density_hbm, density), (basis_hbm, basis), (transfer_hbm, transfer),
            (coupling_hbm, coupling), (far_hbm, far_list), (near_hbm, near_list), (nb_hbm, nb),
        ))
    ]
    for load in loads:
        load.start()

    def at_coef(d):
        return lax.rem(coef + d, nk)

    def at_clus(z, x, c):
        return (z * 2 + x) * 2 + c

    def ring_z(e):
        return lax.rem(zpos + e, outer)

    barrier = pltpu.get_barrier_semaphore()

    def greet(c, k):
        pl.semaphore_signal(barrier, inc=1, device_id=(c, k), device_id_type=MESH)

    for d in range(1, nk):
        greet(clus, at_coef(d))
    for f in range(2):
        for e in range(outer):
            if e + f > 0:
                greet(at_clus(ring_z(e), xpos if f == 0 else 1 - xpos, core), coef)
    greet(at_clus(zpos, xpos, 1 - core), coef)

    @pl.when(clus > 0)
    def _():
        greet(clus - 1, coef)

    @pl.when(clus < nc - 1)
    def _():
        greet(clus + 1, coef)

    pl.semaphore_wait(
        barrier, nk - 1 + 2 * outer + jnp.minimum(clus, 1) + jnp.minimum(nc - 1 - clus, 1)
    )

    def remote(src, dst, ssem, rsem, c, k):
        return pltpu.make_async_remote_copy(
            src_ref=src, dst_ref=dst, send_sem=ssem, recv_sem=rsem,
            device_id=(c, k), device_id_type=MESH,
        )

    def y_copy(a, values, d, chunk):
        start = chunk * NWIN
        return remote(
            values.at[pl.ds(start, NWIN)],
            ext[a].at[pl.ds(NWIN + start, NWIN), my_rows],
            y_send.at[a, d, chunk], y_recv.at[a, d, chunk], clus, at_coef(d),
        )

    def halo_copy(a, values, d, up):
        lo = leaves - NWIN if up else 0
        dst_lo = 0 if up else NWIN + leaves
        owner = lax.rem(coef + nk - d, nk)
        span = pl.ds(pl.multiple_of(owner * rows, rows), rows)
        src = values.at[pl.ds(lo, NWIN)] if d == 0 else ext[a].at[pl.ds(NWIN + lo, NWIN), span]
        side = 1 if up else 0
        return remote(
            src, ext[a].at[pl.ds(dst_lo, NWIN), span],
            h_send.at[a, side, d], h_recv.at[a, side, d], clus + (1 if up else -1), coef,
        )

    def halo_start(a, values, d, up):
        @pl.when((clus < nc - 1) if up else (clus > 0))
        def _():
            halo_copy(a, values, d, up).start()

    def halo_wait_send(a, values, d, up):
        @pl.when((clus < nc - 1) if up else (clus > 0))
        def _():
            halo_copy(a, values, d, up).wait_send()

    def halo_wait_recv(a, values, d, up):
        @pl.when((clus > 0) if up else (clus < nc - 1))
        def _():
            halo_copy(a, values, d, up).wait_recv()

    def piece(a, c):
        return pc[a].at[pl.ds(c * parents, parents)]

    def chip_at(e, f):
        return at_clus(ring_z(e), xpos if f == 0 else 1 - xpos, core)

    def chip_copy(a, e, f):
        return remote(
            piece(a, clus), piece(a, clus), g_ssem.at[a, f, e], g_rsem.at[a, f, e],
            chip_at(e, f), coef,
        )

    def core_copy(a, e, f):
        return remote(
            piece(a, chip_at(e, f)), piece(a, chip_at(e, f)),
            c_ssem.at[a, f, e], c_rsem.at[a, f, e], at_clus(zpos, xpos, 1 - core), coef,
        )

    def rs_copy(a, d):
        to = at_coef(d)
        return remote(
            rs_send.at[a, to], rs_recv.at[a, d], rs_ssem.at[a, d], rs_rsem.at[a, d], clus, to,
        )

    def cp_copy(a, d):
        return remote(
            cp_send.at[a], cp_recv.at[a, d], cp_ssem.at[a, d], cp_rsem.at[a, d], clus, at_coef(d),
        )

    far_first = [(e, f) for e in range(outer - 1, -1, -1) for f in (1, 0) if e + f > 0]
    order = [0, chunks - 1] + list(range(1, chunks - 1))
    offset = clus * leaves - NWIN

    def keep_own(a, values, start, count):
        for i in range(start, start + count):
            ext[a][NWIN + i, my_rows] = values[i]

    def y_start(a, values, chunk):
        for d in range(1, nk):
            y_copy(a, values, d, chunk).start()

    def y_wait(a, values, chunk):
        for d in range(1, nk):
            y_copy(a, values, d, chunk).wait_recv()

    def build_band():
        def leaf(i, carry):
            t, at = i // NWIN, lax.rem(i, NWIN)
            span = pl.ds(pl.multiple_of(at * rows, rows), rows)
            for o in range(2 * NWIN + 1):
                total = jnp.zeros((rows, nb.shape[3]), BF16)
                for k in range(near_k):
                    same = near_list[i, k] == offset + i + o
                    total = total + jnp.where(same, nb[i, k], jnp.zeros_like(total))
                band[t, at + o, span] = total
            for o in range(2 * NWIN + 1, 3 * NWIN):
                band[t, lax.rem(at + o, 3 * NWIN), span] = jnp.zeros((rows, nb.shape[3]), BF16)
            return carry

        lax.fori_loop(0, leaves, leaf, 0)

    def near_from(a, s, seen):
        panel_rows = rows * nk
        source = ext[a][pl.ds((s + 1) * NWIN, NWIN)].reshape(NWIN * panel_rows, vectors)
        for t in (s - 1, s, s + 1):
            if 0 <= t < chunks:
                first_slot = (s - t + 1) * NWIN
                lhs = jnp.concatenate(
                    [band[t, first_slot + n] for n in range(NWIN)], axis=1
                )
                part = jnp.dot(lhs, source, preferred_element_type=F32)
                acc[t] = acc[t] + part if t in seen else part
                seen.add(t)

    def lift(a, values):
        for p in range(parents):
            mine = values[pl.ds(p * CHILD, CHILD)].reshape(CHILD * rows, vectors)
            if a == 0:
                part = lax.dot_general(
                    grow[p], mine, (((0,), (0,)), ((), ())), preferred_element_type=F32
                )
            else:
                part = jnp.dot(grow_t[p], mine, preferred_element_type=F32)
            for o in range(nk):
                rs_send[a, o, p] = part[o * share:(o + 1) * share].astype(BF16)
        for d in range(1, nk):
            rs_copy(a, d).start()

    def middle(a, values):
        total = rs_send[a, coef].astype(F32)
        for d in range(1, nk):
            rs_copy(a, d).wait_recv()
            total = total + rs_recv[a, d].astype(F32)
        pc[a][pl.ds(clus * parents, parents)] = total.astype(BF16)
        for e, f in far_first:
            chip_copy(a, e, f).start()
        core_copy(a, 0, 0).start()
        if a == 1:
            for up in (False, True):
                halo_start(a, values, 0, up)

        if a == 0:
            for load in loads[3:]:
                load.wait()
            for p in range(parents):
                clhs[p] = coupling[p].reshape(far_k * share, rank).T
            for p in range(parents):
                grow_t[p] = grow[p].T
            build_band()

        y_wait(a, values, 0)
        for d in range(1, nk):
            halo_start(a, values, d, False)
        for e, f in far_first[::-1]:
            chip_copy(a, (outer - e) % outer, f).wait_recv()
            core_copy(a, e, f).start()

        y_wait(a, values, chunks - 1)
        for d in range(1, nk):
            halo_start(a, values, d, True)
        seen = set()
        near_from(a, 0, seen)
        near_from(a, chunks - 1, seen)

        for f in range(2):
            for e in range(outer):
                core_copy(a, e, f).wait_recv()
        for p in range(parents):
            picked = jnp.concatenate([pc[a][far_list[p, k]] for k in range(far_k)], axis=0)
            cp_send[a, p] = jnp.dot(clhs[p], picked, preferred_element_type=F32).astype(BF16)
        for d in range(1, nk):
            cp_copy(a, d).start()

        for up, s in ((True, -1), (False, chunks)):
            for d in range(nk):
                halo_wait_recv(a, values, d, up)
            near_from(a, s, seen)
        for s in range(1, chunks - 1):
            y_wait(a, values, s)
            near_from(a, s, seen)

        coupled = cp_send[a].astype(F32)
        for d in range(1, nk):
            cp_copy(a, d).wait_recv()
            coupled = coupled + cp_recv[a, d].astype(F32)
        return coupled.astype(BF16)

    def finish(coupled, result, p):
        far = jnp.dot(grow[p], coupled[p], preferred_element_type=F32)
        span = pl.ds(p * CHILD, CHILD)
        near = acc[pl.ds(p * (CHILD // NWIN), CHILD // NWIN)].reshape(CHILD, rows, vectors)
        result[span] = (near + far.reshape(CHILD, rows, vectors)).astype(BF16)

    loads[0].wait()
    y_start(0, density, order[0])
    for up in (False, True):
        halo_start(0, density, 0, up)
    for n in (1, 2):
        loads[n].wait()

    for i in range(leaves):
        grow[i // CHILD, pl.ds(i % CHILD * rows, rows)] = jnp.dot(
            basis[i], transfer[i], preferred_element_type=F32
        ).astype(BF16)
    lift(0, density)
    for chunk in order[1:]:
        y_start(0, density, chunk)
    keep_own(0, density, 0, leaves)

    @pl.when(clus == 0)
    def _():
        for buffer in ext:
            buffer[pl.ds(0, NWIN)] = jnp.zeros((NWIN,) + buffer.shape[1:], BF16)

    @pl.when(clus == nc - 1)
    def _():
        for buffer in ext:
            buffer[pl.ds(NWIN + leaves, NWIN)] = jnp.zeros((NWIN,) + buffer.shape[1:], BF16)

    coupled = middle(0, density)
    for p in range(parents):
        finish(coupled, first, p)
    lift(1, first)
    for chunk in order:
        y_start(1, first, chunk)
    keep_own(1, first, 0, leaves)

    coupled = middle(1, first)
    for p in range(parents):
        finish(coupled, second, p)

    for a, values in ((0, density), (1, first)):
        for d in range(1, nk):
            rs_copy(a, d).wait_send()
            cp_copy(a, d).wait_send()
            for chunk in range(chunks):
                y_copy(a, values, d, chunk).wait_send()
        for up in (False, True):
            for d in range(nk):
                halo_wait_send(a, values, d, up)
        for e, f in far_first:
            chip_copy(a, e, f).wait_send()
        for f in range(2):
            for e in range(outer):
                core_copy(a, e, f).wait_send()


def hand_over(pieces, first, second, first_out, second_out, held, in_sem, out_sem):
    size = first.shape[0] // pieces
    spans = [(m, n, pl.ds(n * size, size)) for n in range(pieces) for m in range(2)]
    ins = [
        pltpu.make_async_copy((first, second)[m].at[span], held.at[m, span], in_sem.at[m, n])
        for m, n, span in spans
    ]
    outs = [
        pltpu.make_async_copy(
            held.at[m, span], (first_out, second_out)[m].at[span], out_sem.at[m, n]
        )
        for m, n, span in spans
    ]
    for copy in ins:
        copy.start()
    for came, goes in zip(ins, outs):
        came.wait()
        goes.start()
    for copy in outs:
        copy.wait()


def body(nc, nk, density, near_list, far_list, near_blocks, basis, transfer, coupling):
    coupling = jnp.swapaxes(coupling, 2, 3)
    leaves, rows, vectors = density.shape
    parents = leaves // CHILD
    share, rank = coupling.shape[2:]
    far_k = coupling.shape[1]
    outer = nc // 4
    chunks = leaves // NWIN
    vmem = pl.BlockSpec(memory_space=pltpu.VMEM)
    anywhere = pl.BlockSpec(memory_space=pl.ANY)
    dma = pltpu.SemaphoreType.DMA
    held = pl.pallas_call(
        functools.partial(kernel, nc, nk),
        out_shape=(jax.ShapeDtypeStruct(density.shape, BF16),) * 2,
        in_specs=[anywhere] * 7,
        out_specs=(vmem, vmem),
        scratch_shapes=[
            pltpu.VMEM(density.shape, BF16),
            pltpu.SMEM(near_list.shape, jnp.int32),
            pltpu.SMEM(far_list.shape, jnp.int32),
            pltpu.VMEM(near_blocks.shape, BF16),
            pltpu.VMEM(basis.shape, BF16),
            pltpu.VMEM(transfer.shape, BF16),
            pltpu.VMEM(coupling.shape, BF16),
            pltpu.VMEM((parents, rank, far_k * share), BF16),
            pltpu.VMEM((parents, CHILD * rows, rank), BF16),
            pltpu.VMEM((parents, rank, CHILD * rows), BF16),
            pltpu.VMEM((leaves + 2 * NWIN, rows * nk, vectors), BF16),
            pltpu.VMEM((leaves + 2 * NWIN, rows * nk, vectors), BF16),
            pltpu.VMEM((chunks, 3 * NWIN, NWIN * rows, near_blocks.shape[3]), BF16),
            pltpu.VMEM((2, nk, parents, share, vectors), BF16),
            pltpu.VMEM((2, nk, parents, share, vectors), BF16),
            pltpu.VMEM((nc * parents, share, vectors), BF16),
            pltpu.VMEM((nc * parents, share, vectors), BF16),
            pltpu.VMEM((2, parents, rank, vectors), BF16),
            pltpu.VMEM((2, nk, parents, rank, vectors), BF16),
            pltpu.VMEM((chunks, NWIN * rows, vectors), F32),
            dma((7,)),
            dma((2, nk, chunks)),
            dma((2, nk, chunks)),
            dma((2, 2, nk)),
            dma((2, 2, nk)),
            dma((2, nk)),
            dma((2, nk)),
            dma((2, 2, outer)),
            dma((2, 2, outer)),
            dma((2, 2, outer)),
            dma((2, 2, outer)),
            dma((2, nk)),
            dma((2, nk)),
        ],
        compiler_params=pltpu.CompilerParams(
            collective_id=0, has_side_effects=True, vmem_limit_bytes=56 * 1024 * 1024
        ),
        cost_estimate=pl.CostEstimate(
            flops=4 * near_blocks.size * vectors, bytes_accessed=2 * near_blocks.size,
            transcendentals=0,
        ),
    )(density, near_list, far_list, near_blocks, basis, transfer, coupling)
    return pl.pallas_call(
        functools.partial(hand_over, chunks // 2),
        out_shape=(jax.ShapeDtypeStruct(density.shape, BF16),) * 2,
        in_specs=[anywhere] * 2,
        out_specs=(anywhere,) * 2,
        scratch_shapes=[
            pltpu.VMEM((2,) + density.shape, BF16), dma((2, chunks)), dma((2, chunks)),
        ],
        compiler_params=pltpu.CompilerParams(vmem_limit_bytes=56 * 1024 * 1024),
    )(*held)


def solution(mesh):
    placed = (
        P("clus", "coef", None),
        P("clus", None),
        P("clus", None),
        P("clus", None, "coef", None),
        P("clus", "coef", None),
        P("clus", None, None),
        P("clus", None, None, "coef"),
    )
    return jax.shard_map(
        functools.partial(body, mesh.shape["clus"], mesh.shape["coef"]),
        mesh=mesh,
        in_specs=placed,
        out_specs=(P("clus", "coef", None), P("clus", "coef", None)),
        check_vma=False,
    )
```

```python
import functools

import jax
import jax.numpy as jnp
from jax import lax
from jax.experimental import pallas as pl
from jax.experimental.pallas import tpu as pltpu
from jax.sharding import PartitionSpec as P

CHILD = 8
NWIN = 4
MESH = pl.DeviceIdType.MESH
F32 = jnp.float32
BF16 = jnp.bfloat16


def kernel(
    nc, nk,
    density_hbm, near_hbm, far_hbm, nb_hbm, basis_hbm, transfer_hbm, coupling_hbm,
    first, second,
    density, near_list, far_list, nb, basis, transfer, coupling,
    clhs, grow, grow_t, ext_a, ext_b, band, rs_send, rs_recv, pc_a0, pc_a1, pc_b0, pc_b1, cp_send, cp_recv, acc,
    load_sem, y_send, y_recv, h_send, h_recv, rs_ssem, rs_rsem,
    g_ssem, g_rsem, c_ssem, c_rsem, cp_ssem, cp_rsem,
):
    leaves, rows, vectors = density.shape
    parents = leaves // CHILD
    near_k = nb.shape[1]
    far_k = coupling.shape[1]
    share = coupling.shape[2]
    rank = grow.shape[2]
    outer = nc // 4
    chunks = leaves // NWIN
    clus = lax.axis_index("clus")
    coef = lax.axis_index("coef")
    core = lax.rem(clus, 2)
    xpos = lax.rem(clus // 2, 2)
    zpos = clus // 4
    ext = (ext_a, ext_b)
    half = vectors // 2
    part_of = [pl.ds(v * half, half) for v in range(2)]
    pc = ((pc_a0, pc_a1), (pc_b0, pc_b1))
    my_rows = pl.ds(pl.multiple_of(coef * rows, rows), rows)

    loads = [
        pltpu.make_async_copy(src, dst, load_sem.at[n])
        for n, (src, dst) in enumerate((
            (density_hbm, density), (basis_hbm, basis), (transfer_hbm, transfer),
            (coupling_hbm, coupling), (far_hbm, far_list), (near_hbm, near_list), (nb_hbm, nb),
        ))
    ]
    for load in loads:
        load.start()

    def at_coef(d):
        return lax.rem(coef + d, nk)

    def at_clus(z, x, c):
        return (z * 2 + x) * 2 + c

    def ring_z(e):
        return lax.rem(zpos + e, outer)

    barrier = pltpu.get_barrier_semaphore()

    def greet(c, k):
        pl.semaphore_signal(barrier, inc=1, device_id=(c, k), device_id_type=MESH)

    for d in range(1, nk):
        greet(clus, at_coef(d))
    for f in range(2):
        for e in range(outer):
            if e + f > 0:
                greet(at_clus(ring_z(e), xpos if f == 0 else 1 - xpos, core), coef)
    greet(at_clus(zpos, xpos, 1 - core), coef)

    @pl.when(clus > 0)
    def _():
        greet(clus - 1, coef)

    @pl.when(clus < nc - 1)
    def _():
        greet(clus + 1, coef)

    pl.semaphore_wait(
        barrier, nk - 1 + 2 * outer + jnp.minimum(clus, 1) + jnp.minimum(nc - 1 - clus, 1)
    )

    def remote(src, dst, ssem, rsem, c, k):
        return pltpu.make_async_remote_copy(
            src_ref=src, dst_ref=dst, send_sem=ssem, recv_sem=rsem,
            device_id=(c, k), device_id_type=MESH,
        )

    def y_copy(a, values, d, chunk):
        start = chunk * NWIN
        return remote(
            values.at[pl.ds(start, NWIN)],
            ext[a].at[pl.ds(NWIN + start, NWIN), my_rows],
            y_send.at[a, d, chunk], y_recv.at[a, d, chunk], clus, at_coef(d),
        )

    def halo_copy(a, values, d, up):
        lo = leaves - NWIN if up else 0
        dst_lo = 0 if up else NWIN + leaves
        owner = lax.rem(coef + nk - d, nk)
        span = pl.ds(pl.multiple_of(owner * rows, rows), rows)
        src = values.at[pl.ds(lo, NWIN)] if d == 0 else ext[a].at[pl.ds(NWIN + lo, NWIN), span]
        side = 1 if up else 0
        return remote(
            src, ext[a].at[pl.ds(dst_lo, NWIN), span],
            h_send.at[a, side, d], h_recv.at[a, side, d], clus + (1 if up else -1), coef,
        )

    def halo_start(a, values, d, up):
        @pl.when((clus < nc - 1) if up else (clus > 0))
        def _():
            halo_copy(a, values, d, up).start()

    def halo_wait_send(a, values, d, up):
        @pl.when((clus < nc - 1) if up else (clus > 0))
        def _():
            halo_copy(a, values, d, up).wait_send()

    def halo_wait_recv(a, values, d, up):
        @pl.when((clus > 0) if up else (clus < nc - 1))
        def _():
            halo_copy(a, values, d, up).wait_recv()

    def piece(a, c, v):
        return pc[a][v].at[pl.ds(c * parents, parents)]

    def chip_at(e, f):
        return at_clus(ring_z(e), xpos if f == 0 else 1 - xpos, core)

    def chip_copy(a, e, f, v):
        return remote(
            piece(a, clus, v), piece(a, clus, v), g_ssem.at[a, v, f, e], g_rsem.at[a, v, f, e],
            chip_at(e, f), coef,
        )

    def core_copy(a, e, f, v):
        return remote(
            piece(a, chip_at(e, f), v), piece(a, chip_at(e, f), v),
            c_ssem.at[a, v, f, e], c_rsem.at[a, v, f, e], at_clus(zpos, xpos, 1 - core), coef,
        )

    def rs_copy(a, d, v):
        to = at_coef(d)
        return remote(
            rs_send.at[a, to, :, :, part_of[v]], rs_recv.at[a, d, :, :, part_of[v]],
            rs_ssem.at[a, v, d], rs_rsem.at[a, v, d], clus, to,
        )

    def cp_copy(a, d, v):
        return remote(
            cp_send.at[a, :, :, part_of[v]], cp_recv.at[a, d, :, :, part_of[v]],
            cp_ssem.at[a, v, d], cp_rsem.at[a, v, d], clus, at_coef(d),
        )

    far_first = [(e, f) for e in range(outer - 1, -1, -1) for f in (1, 0) if e + f > 0]
    order = [0, chunks - 1] + list(range(1, chunks - 1))
    offset = clus * leaves - NWIN

    def keep_own(a, values, start, count):
        for i in range(start, start + count):
            ext[a][NWIN + i, my_rows] = values[i]

    def y_start(a, values, chunk):
        for d in range(1, nk):
            y_copy(a, values, d, chunk).start()

    def y_wait(a, values, chunk):
        for d in range(1, nk):
            y_copy(a, values, d, chunk).wait_recv()

    def build_band(start, stop):
        def leaf(i, carry):
            t, at = i // NWIN, lax.rem(i, NWIN)
            span = pl.ds(pl.multiple_of(at * rows, rows), rows)
            for o in range(2 * NWIN + 1):
                total = jnp.zeros((rows, nb.shape[3]), BF16)
                for k in range(near_k):
                    same = near_list[i, k] == offset + i + o
                    total = total + jnp.where(same, nb[i, k], jnp.zeros_like(total))
                band[t, at + o, span] = total
            for o in range(2 * NWIN + 1, 3 * NWIN):
                band[t, lax.rem(at + o, 3 * NWIN), span] = jnp.zeros((rows, nb.shape[3]), BF16)
            return carry

        lax.fori_loop(start, stop, leaf, 0)

    def near_from(a, s, seen):
        panel_rows = rows * nk
        source = ext[a][pl.ds((s + 1) * NWIN, NWIN)].reshape(NWIN * panel_rows, vectors)
        for t in (s - 1, s, s + 1):
            if 0 <= t < chunks:
                first_slot = (s - t + 1) * NWIN
                lhs = jnp.concatenate(
                    [band[t, first_slot + n] for n in range(NWIN)], axis=1
                )
                part = jnp.dot(lhs, source, preferred_element_type=F32)
                acc[t] = acc[t] + part if t in seen else part
                seen.add(t)

    def lift(a, values):
        for p in range(parents):
            mine = values[pl.ds(p * CHILD, CHILD)].reshape(CHILD * rows, vectors)
            if a == 0:
                part = lax.dot_general(
                    grow[p], mine, (((0,), (0,)), ((), ())), preferred_element_type=F32
                )
            else:
                part = jnp.dot(grow_t[p], mine, preferred_element_type=F32)
            for o in range(nk):
                rs_send[a, o, p] = part[o * share:(o + 1) * share].astype(BF16)
        for v in range(2):
            for d in range(1, nk):
                rs_copy(a, d, v).start()

    def middle(a, values):
        if a == 0:
            for load in loads[3:]:
                load.wait()
            build_band(0, leaves // 2)
        for v in range(2):
            total = rs_send[a, coef, :, :, part_of[v]].astype(F32)
            for d in range(1, nk):
                rs_copy(a, d, v).wait_recv()
                total = total + rs_recv[a, d, :, :, part_of[v]].astype(F32)
            pc[a][v][pl.ds(clus * parents, parents)] = total.astype(BF16)
            for e, f in far_first:
                chip_copy(a, e, f, v).start()
            core_copy(a, 0, 0, v).start()
        if a == 1:
            for up in (False, True):
                halo_start(a, values, 0, up)

        if a == 0:
            for p in range(parents):
                clhs[p] = coupling[p].reshape(far_k * share, rank).T
            for p in range(parents):
                grow_t[p] = grow[p].T
            build_band(leaves // 2, leaves)

        y_wait(a, values, 0)
        for d in range(1, nk):
            halo_start(a, values, d, False)
        seen = set()
        for v in range(2):
            for e, f in far_first[::-1]:
                chip_copy(a, (outer - e) % outer, f, v).wait_recv()
                core_copy(a, e, f, v).start()
            if v == 1:
                y_wait(a, values, chunks - 1)
                for d in range(1, nk):
                    halo_start(a, values, d, True)
                near_from(a, 0, seen)
                near_from(a, chunks - 1, seen)
            for f in range(2):
                for e in range(outer):
                    core_copy(a, e, f, v).wait_recv()
            for p in range(parents):
                picked = jnp.concatenate(
                    [pc[a][v][far_list[p, k]] for k in range(far_k)], axis=0
                )
                cp_send[a, p, :, part_of[v]] = jnp.dot(
                    clhs[p], picked, preferred_element_type=F32
                ).astype(BF16)
            for d in range(1, nk):
                cp_copy(a, d, v).start()

        for up, s in ((True, -1), (False, chunks)):
            for d in range(nk):
                halo_wait_recv(a, values, d, up)
            near_from(a, s, seen)
        for s in range(1, chunks - 1):
            y_wait(a, values, s)
            near_from(a, s, seen)

        for v in range(2):
            for d in range(1, nk):
                cp_copy(a, d, v).wait_recv()
        coupled = cp_send[a].astype(F32)
        for d in range(1, nk):
            coupled = coupled + cp_recv[a, d].astype(F32)
        return coupled.astype(BF16)

    def finish(coupled, result, p):
        far = jnp.dot(grow[p], coupled[p], preferred_element_type=F32)
        span = pl.ds(p * CHILD, CHILD)
        near = acc[pl.ds(p * (CHILD // NWIN), CHILD // NWIN)].reshape(CHILD, rows, vectors)
        result[span] = (near + far.reshape(CHILD, rows, vectors)).astype(BF16)

    loads[0].wait()
    y_start(0, density, order[0])
    for up in (False, True):
        halo_start(0, density, 0, up)
    for n in (1, 2):
        loads[n].wait()

    for i in range(leaves):
        grow[i // CHILD, pl.ds(i % CHILD * rows, rows)] = jnp.dot(
            basis[i], transfer[i], preferred_element_type=F32
        ).astype(BF16)
    lift(0, density)
    for chunk in order[1:]:
        y_start(0, density, chunk)
    keep_own(0, density, 0, leaves)

    @pl.when(clus == 0)
    def _():
        for buffer in ext:
            buffer[pl.ds(0, NWIN)] = jnp.zeros((NWIN,) + buffer.shape[1:], BF16)

    @pl.when(clus == nc - 1)
    def _():
        for buffer in ext:
            buffer[pl.ds(NWIN + leaves, NWIN)] = jnp.zeros((NWIN,) + buffer.shape[1:], BF16)

    coupled = middle(0, density)
    for p in range(parents):
        finish(coupled, first, p)
    lift(1, first)
    for chunk in order:
        y_start(1, first, chunk)
    keep_own(1, first, 0, leaves)

    coupled = middle(1, first)
    for p in range(parents):
        finish(coupled, second, p)

    for a, values in ((0, density), (1, first)):
        for d in range(1, nk):
            for v in range(2):
                rs_copy(a, d, v).wait_send()
                cp_copy(a, d, v).wait_send()
            for chunk in range(chunks):
                y_copy(a, values, d, chunk).wait_send()
        for up in (False, True):
            for d in range(nk):
                halo_wait_send(a, values, d, up)
        for v in range(2):
            for e, f in far_first:
                chip_copy(a, e, f, v).wait_send()
            for f in range(2):
                for e in range(outer):
                    core_copy(a, e, f, v).wait_send()


def hand_over(pieces, first, second, first_out, second_out, held, in_sem, out_sem):
    size = first.shape[0] // pieces
    spans = [(m, n, pl.ds(n * size, size)) for n in range(pieces) for m in range(2)]
    ins = [
        pltpu.make_async_copy((first, second)[m].at[span], held.at[m, span], in_sem.at[m, n])
        for m, n, span in spans
    ]
    outs = [
        pltpu.make_async_copy(
            held.at[m, span], (first_out, second_out)[m].at[span], out_sem.at[m, n]
        )
        for m, n, span in spans
    ]
    for copy in ins:
        copy.start()
    for came, goes in zip(ins, outs):
        came.wait()
        goes.start()
    for copy in outs:
        copy.wait()


def body(nc, nk, density, near_list, far_list, near_blocks, basis, transfer, coupling):
    coupling = jnp.swapaxes(coupling, 2, 3)
    leaves, rows, vectors = density.shape
    parents = leaves // CHILD
    share, rank = coupling.shape[2:]
    far_k = coupling.shape[1]
    outer = nc // 4
    chunks = leaves // NWIN
    vmem = pl.BlockSpec(memory_space=pltpu.VMEM)
    anywhere = pl.BlockSpec(memory_space=pl.ANY)
    dma = pltpu.SemaphoreType.DMA
    held = pl.pallas_call(
        functools.partial(kernel, nc, nk),
        out_shape=(jax.ShapeDtypeStruct(density.shape, BF16),) * 2,
        in_specs=[anywhere] * 7,
        out_specs=(vmem, vmem),
        scratch_shapes=[
            pltpu.VMEM(density.shape, BF16),
            pltpu.SMEM(near_list.shape, jnp.int32),
            pltpu.SMEM(far_list.shape, jnp.int32),
            pltpu.VMEM(near_blocks.shape, BF16),
            pltpu.VMEM(basis.shape, BF16),
            pltpu.VMEM(transfer.shape, BF16),
            pltpu.VMEM(coupling.shape, BF16),
            pltpu.VMEM((parents, rank, far_k * share), BF16),
            pltpu.VMEM((parents, CHILD * rows, rank), BF16),
            pltpu.VMEM((parents, rank, CHILD * rows), BF16),
            pltpu.VMEM((leaves + 2 * NWIN, rows * nk, vectors), BF16),
            pltpu.VMEM((leaves + 2 * NWIN, rows * nk, vectors), BF16),
            pltpu.VMEM((chunks, 3 * NWIN, NWIN * rows, near_blocks.shape[3]), BF16),
            pltpu.VMEM((2, nk, parents, share, vectors), BF16),
            pltpu.VMEM((2, nk, parents, share, vectors), BF16),
            *[pltpu.VMEM((nc * parents, share, vectors // 2), BF16)] * 4,
            pltpu.VMEM((2, parents, rank, vectors), BF16),
            pltpu.VMEM((2, nk, parents, rank, vectors), BF16),
            pltpu.VMEM((chunks, NWIN * rows, vectors), F32),
            dma((7,)),
            dma((2, nk, chunks)),
            dma((2, nk, chunks)),
            dma((2, 2, nk)),
            dma((2, 2, nk)),
            dma((2, 2, nk)),
            dma((2, 2, nk)),
            dma((2, 2, 2, outer)),
            dma((2, 2, 2, outer)),
            dma((2, 2, 2, outer)),
            dma((2, 2, 2, outer)),
            dma((2, 2, nk)),
            dma((2, 2, nk)),
        ],
        compiler_params=pltpu.CompilerParams(
            collective_id=0, has_side_effects=True, vmem_limit_bytes=56 * 1024 * 1024
        ),
        cost_estimate=pl.CostEstimate(
            flops=4 * near_blocks.size * vectors, bytes_accessed=2 * near_blocks.size,
            transcendentals=0,
        ),
    )(density, near_list, far_list, near_blocks, basis, transfer, coupling)
    return pl.pallas_call(
        functools.partial(hand_over, chunks // 2),
        out_shape=(jax.ShapeDtypeStruct(density.shape, BF16),) * 2,
        in_specs=[anywhere] * 2,
        out_specs=(anywhere,) * 2,
        scratch_shapes=[
            pltpu.VMEM((2,) + density.shape, BF16), dma((2, chunks)), dma((2, chunks)),
        ],
        compiler_params=pltpu.CompilerParams(vmem_limit_bytes=56 * 1024 * 1024),
    )(*held)


def solution(mesh):
    placed = (
        P("clus", "coef", None),
        P("clus", None),
        P("clus", None),
        P("clus", None, "coef", None),
        P("clus", "coef", None),
        P("clus", None, None),
        P("clus", None, None, "coef"),
    )
    return jax.shard_map(
        functools.partial(body, mesh.shape["clus"], mesh.shape["coef"]),
        mesh=mesh,
        in_specs=placed,
        out_specs=(P("clus", "coef", None), P("clus", "coef", None)),
        check_vma=False,
    )
```

```python
import functools

import jax
import jax.numpy as jnp
from jax import lax
from jax.experimental import pallas as pl
from jax.experimental.pallas import tpu as pltpu
from jax.sharding import PartitionSpec as P

CHILD = 8
NWIN = 4
MESH = pl.DeviceIdType.MESH
F32 = jnp.float32
BF16 = jnp.bfloat16


def kernel(
    nc, nk,
    density_hbm, near_hbm, far_hbm, nb_hbm, basis_hbm, transfer_hbm, coupling_hbm,
    first_out, second,
    first, density, near_list, far_list, nb, basis, transfer, coupling,
    clhs, grow, grow_t, ext_a, ext_b, band, rs_send, rs_recv, pc_a0, pc_a1, pc_b0, pc_b1, cp_send, cp_recv, acc,
    load_sem, out_sem, y_send, y_recv, h_send, h_recv, rs_ssem, rs_rsem,
    g_ssem, g_rsem, c_ssem, c_rsem, cp_ssem, cp_rsem,
):
    leaves, rows, vectors = density.shape
    parents = leaves // CHILD
    near_k = nb.shape[1]
    far_k = coupling.shape[1]
    share = coupling.shape[2]
    rank = grow.shape[2]
    outer = nc // 4
    chunks = leaves // NWIN
    clus = lax.axis_index("clus")
    coef = lax.axis_index("coef")
    core = lax.rem(clus, 2)
    xpos = lax.rem(clus // 2, 2)
    zpos = clus // 4
    ext = (ext_a, ext_b)
    half = vectors // 2
    part_of = [pl.ds(v * half, half) for v in range(2)]
    pc = ((pc_a0, pc_a1), (pc_b0, pc_b1))
    my_rows = pl.ds(pl.multiple_of(coef * rows, rows), rows)

    loads = [
        pltpu.make_async_copy(src, dst, load_sem.at[n])
        for n, (src, dst) in enumerate((
            (density_hbm, density), (basis_hbm, basis), (transfer_hbm, transfer),
            (coupling_hbm, coupling), (far_hbm, far_list), (near_hbm, near_list), (nb_hbm, nb),
        ))
    ]
    for load in loads:
        load.start()

    def at_coef(d):
        return lax.rem(coef + d, nk)

    def at_clus(z, x, c):
        return (z * 2 + x) * 2 + c

    def ring_z(e):
        return lax.rem(zpos + e, outer)

    barrier = pltpu.get_barrier_semaphore()

    def greet(c, k):
        pl.semaphore_signal(barrier, inc=1, device_id=(c, k), device_id_type=MESH)

    for d in range(1, nk):
        greet(clus, at_coef(d))
    for f in range(2):
        for e in range(outer):
            if e + f > 0:
                greet(at_clus(ring_z(e), xpos if f == 0 else 1 - xpos, core), coef)
    greet(at_clus(zpos, xpos, 1 - core), coef)

    @pl.when(clus > 0)
    def _():
        greet(clus - 1, coef)

    @pl.when(clus < nc - 1)
    def _():
        greet(clus + 1, coef)

    pl.semaphore_wait(
        barrier, nk - 1 + 2 * outer + jnp.minimum(clus, 1) + jnp.minimum(nc - 1 - clus, 1)
    )

    def remote(src, dst, ssem, rsem, c, k):
        return pltpu.make_async_remote_copy(
            src_ref=src, dst_ref=dst, send_sem=ssem, recv_sem=rsem,
            device_id=(c, k), device_id_type=MESH,
        )

    def y_copy(a, values, d, chunk):
        start = chunk * NWIN
        return remote(
            values.at[pl.ds(start, NWIN)],
            ext[a].at[pl.ds(NWIN + start, NWIN), my_rows],
            y_send.at[a, d, chunk], y_recv.at[a, d, chunk], clus, at_coef(d),
        )

    def halo_copy(a, values, d, up):
        lo = leaves - NWIN if up else 0
        dst_lo = 0 if up else NWIN + leaves
        owner = lax.rem(coef + nk - d, nk)
        span = pl.ds(pl.multiple_of(owner * rows, rows), rows)
        src = values.at[pl.ds(lo, NWIN)] if d == 0 else ext[a].at[pl.ds(NWIN + lo, NWIN), span]
        side = 1 if up else 0
        return remote(
            src, ext[a].at[pl.ds(dst_lo, NWIN), span],
            h_send.at[a, side, d], h_recv.at[a, side, d], clus + (1 if up else -1), coef,
        )

    def halo_start(a, values, d, up):
        @pl.when((clus < nc - 1) if up else (clus > 0))
        def _():
            halo_copy(a, values, d, up).start()

    def halo_wait_send(a, values, d, up):
        @pl.when((clus < nc - 1) if up else (clus > 0))
        def _():
            halo_copy(a, values, d, up).wait_send()

    def halo_wait_recv(a, values, d, up):
        @pl.when((clus > 0) if up else (clus < nc - 1))
        def _():
            halo_copy(a, values, d, up).wait_recv()

    def piece(a, c, v):
        return pc[a][v].at[pl.ds(c * parents, parents)]

    def chip_at(e, f):
        return at_clus(ring_z(e), xpos if f == 0 else 1 - xpos, core)

    def chip_copy(a, e, f, v):
        return remote(
            piece(a, clus, v), piece(a, clus, v), g_ssem.at[a, v, f, e], g_rsem.at[a, v, f, e],
            chip_at(e, f), coef,
        )

    def core_copy(a, e, f, v):
        return remote(
            piece(a, chip_at(e, f), v), piece(a, chip_at(e, f), v),
            c_ssem.at[a, v, f, e], c_rsem.at[a, v, f, e], at_clus(zpos, xpos, 1 - core), coef,
        )

    def rs_copy(a, d, v):
        to = at_coef(d)
        return remote(
            rs_send.at[a, to, :, :, part_of[v]], rs_recv.at[a, d, :, :, part_of[v]],
            rs_ssem.at[a, v, d], rs_rsem.at[a, v, d], clus, to,
        )

    def cp_copy(a, d, v):
        return remote(
            cp_send.at[a, :, :, part_of[v]], cp_recv.at[a, d, :, :, part_of[v]],
            cp_ssem.at[a, v, d], cp_rsem.at[a, v, d], clus, at_coef(d),
        )

    far_first = [(e, f) for e in range(outer - 1, -1, -1) for f in (1, 0) if e + f > 0]
    order = [0, chunks - 1] + list(range(1, chunks - 1))
    offset = clus * leaves - NWIN

    def keep_own(a, values, start, count):
        for i in range(start, start + count):
            ext[a][NWIN + i, my_rows] = values[i]

    def y_start(a, values, chunk):
        for d in range(1, nk):
            y_copy(a, values, d, chunk).start()

    def y_wait(a, values, chunk):
        for d in range(1, nk):
            y_copy(a, values, d, chunk).wait_recv()

    def build_band(start, stop):
        def leaf(i, carry):
            t, at = i // NWIN, lax.rem(i, NWIN)
            span = pl.ds(pl.multiple_of(at * rows, rows), rows)
            for o in range(2 * NWIN + 1):
                total = jnp.zeros((rows, nb.shape[3]), BF16)
                for k in range(near_k):
                    same = near_list[i, k] == offset + i + o
                    total = total + jnp.where(same, nb[i, k], jnp.zeros_like(total))
                band[t, at + o, span] = total
            for o in range(2 * NWIN + 1, 3 * NWIN):
                band[t, lax.rem(at + o, 3 * NWIN), span] = jnp.zeros((rows, nb.shape[3]), BF16)
            return carry

        lax.fori_loop(start, stop, leaf, 0)

    def near_from(a, s, seen):
        panel_rows = rows * nk
        source = ext[a][pl.ds((s + 1) * NWIN, NWIN)].reshape(NWIN * panel_rows, vectors)
        for t in (s - 1, s, s + 1):
            if 0 <= t < chunks:
                first_slot = (s - t + 1) * NWIN
                lhs = jnp.concatenate(
                    [band[t, first_slot + n] for n in range(NWIN)], axis=1
                )
                part = jnp.dot(lhs, source, preferred_element_type=F32)
                acc[t] = acc[t] + part if t in seen else part
                seen.add(t)

    def lift(a, values):
        for p in range(parents):
            mine = values[pl.ds(p * CHILD, CHILD)].reshape(CHILD * rows, vectors)
            if a == 0:
                part = lax.dot_general(
                    grow[p], mine, (((0,), (0,)), ((), ())), preferred_element_type=F32
                )
            else:
                part = jnp.dot(grow_t[p], mine, preferred_element_type=F32)
            for o in range(nk):
                rs_send[a, o, p] = part[o * share:(o + 1) * share].astype(BF16)
        for v in range(2):
            for d in range(1, nk):
                rs_copy(a, d, v).start()

    def middle(a, values):
        if a == 0:
            for load in loads[3:]:
                load.wait()
            build_band(0, leaves // 2)
        for v in range(2):
            total = rs_send[a, coef, :, :, part_of[v]].astype(F32)
            for d in range(1, nk):
                rs_copy(a, d, v).wait_recv()
                total = total + rs_recv[a, d, :, :, part_of[v]].astype(F32)
            pc[a][v][pl.ds(clus * parents, parents)] = total.astype(BF16)
            for e, f in far_first:
                chip_copy(a, e, f, v).start()
            core_copy(a, 0, 0, v).start()
        if a == 1:
            for up in (False, True):
                halo_start(a, values, 0, up)

        if a == 0:
            for p in range(parents):
                clhs[p] = coupling[p].reshape(far_k * share, rank).T
            for p in range(parents):
                grow_t[p] = grow[p].T
            build_band(leaves // 2, leaves)

        y_wait(a, values, 0)
        for d in range(1, nk):
            halo_start(a, values, d, False)
        seen = set()
        for v in range(2):
            for e, f in far_first[::-1]:
                chip_copy(a, (outer - e) % outer, f, v).wait_recv()
                core_copy(a, e, f, v).start()
            if v == 1:
                near_from(a, 0, seen)
            for f in range(2):
                for e in range(outer):
                    core_copy(a, e, f, v).wait_recv()
            for p in range(parents):
                picked = jnp.concatenate(
                    [pc[a][v][far_list[p, k]] for k in range(far_k)], axis=0
                )
                cp_send[a, p, :, part_of[v]] = jnp.dot(
                    clhs[p], picked, preferred_element_type=F32
                ).astype(BF16)
            for d in range(1, nk):
                cp_copy(a, d, v).start()

        y_wait(a, values, chunks - 1)
        for d in range(1, nk):
            halo_start(a, values, d, True)
        near_from(a, chunks - 1, seen)
        for up, s in ((True, -1), (False, chunks)):
            for d in range(nk):
                halo_wait_recv(a, values, d, up)
            near_from(a, s, seen)
        for s in range(1, chunks - 1):
            y_wait(a, values, s)
            near_from(a, s, seen)

        for v in range(2):
            for d in range(1, nk):
                cp_copy(a, d, v).wait_recv()
        coupled = cp_send[a].astype(F32)
        for d in range(1, nk):
            coupled = coupled + cp_recv[a, d].astype(F32)
        return coupled.astype(BF16)

    def finish(coupled, result, p):
        far = jnp.dot(grow[p], coupled[p], preferred_element_type=F32)
        span = pl.ds(p * CHILD, CHILD)
        near = acc[pl.ds(p * (CHILD // NWIN), CHILD // NWIN)].reshape(CHILD, rows, vectors)
        result[span] = (near + far.reshape(CHILD, rows, vectors)).astype(BF16)

    loads[0].wait()
    y_start(0, density, order[0])
    for up in (False, True):
        halo_start(0, density, 0, up)
    for n in (1, 2):
        loads[n].wait()

    for i in range(leaves):
        grow[i // CHILD, pl.ds(i % CHILD * rows, rows)] = jnp.dot(
            basis[i], transfer[i], preferred_element_type=F32
        ).astype(BF16)
    lift(0, density)
    for chunk in order[1:]:
        y_start(0, density, chunk)
    keep_own(0, density, 0, leaves)

    @pl.when(clus == 0)
    def _():
        for buffer in ext:
            buffer[pl.ds(0, NWIN)] = jnp.zeros((NWIN,) + buffer.shape[1:], BF16)

    @pl.when(clus == nc - 1)
    def _():
        for buffer in ext:
            buffer[pl.ds(NWIN + leaves, NWIN)] = jnp.zeros((NWIN,) + buffer.shape[1:], BF16)

    coupled = middle(0, density)
    for p in range(parents):
        finish(coupled, first, p)
    lift(1, first)
    for chunk in order:
        y_start(1, first, chunk)
    keep_own(1, first, 0, leaves)
    leave = pltpu.make_async_copy(first, first_out, out_sem)
    leave.start()

    coupled = middle(1, first)
    for p in range(parents):
        finish(coupled, second, p)
    leave.wait()

    for a, values in ((0, density), (1, first)):
        for d in range(1, nk):
            for v in range(2):
                rs_copy(a, d, v).wait_send()
                cp_copy(a, d, v).wait_send()
            for chunk in range(chunks):
                y_copy(a, values, d, chunk).wait_send()
        for up in (False, True):
            for d in range(nk):
                halo_wait_send(a, values, d, up)
        for v in range(2):
            for e, f in far_first:
                chip_copy(a, e, f, v).wait_send()
            for f in range(2):
                for e in range(outer):
                    core_copy(a, e, f, v).wait_send()


def hand_over(pieces, first, second, first_out, second_out, held, in_sem, out_sem):
    size = first.shape[0] // pieces
    spans = [(m, n, pl.ds(n * size, size)) for n in range(pieces) for m in range(2)]
    ins = [
        pltpu.make_async_copy((first, second)[m].at[span], held.at[m, span], in_sem.at[m, n])
        for m, n, span in spans
    ]
    outs = [
        pltpu.make_async_copy(
            held.at[m, span], (first_out, second_out)[m].at[span], out_sem.at[m, n]
        )
        for m, n, span in spans
    ]
    for copy in ins:
        copy.start()
    for came, goes in zip(ins, outs):
        came.wait()
        goes.start()
    for copy in outs:
        copy.wait()


def body(nc, nk, density, near_list, far_list, near_blocks, basis, transfer, coupling):
    coupling = jnp.swapaxes(coupling, 2, 3)
    leaves, rows, vectors = density.shape
    parents = leaves // CHILD
    share, rank = coupling.shape[2:]
    far_k = coupling.shape[1]
    outer = nc // 4
    chunks = leaves // NWIN
    vmem = pl.BlockSpec(memory_space=pltpu.VMEM)
    anywhere = pl.BlockSpec(memory_space=pl.ANY)
    dma = pltpu.SemaphoreType.DMA
    held = pl.pallas_call(
        functools.partial(kernel, nc, nk),
        out_shape=(jax.ShapeDtypeStruct(density.shape, BF16),) * 2,
        in_specs=[anywhere] * 7,
        out_specs=(anywhere, vmem),
        scratch_shapes=[
            pltpu.VMEM(density.shape, BF16),
            pltpu.VMEM(density.shape, BF16),
            pltpu.SMEM(near_list.shape, jnp.int32),
            pltpu.SMEM(far_list.shape, jnp.int32),
            pltpu.VMEM(near_blocks.shape, BF16),
            pltpu.VMEM(basis.shape, BF16),
            pltpu.VMEM(transfer.shape, BF16),
            pltpu.VMEM(coupling.shape, BF16),
            pltpu.VMEM((parents, rank, far_k * share), BF16),
            pltpu.VMEM((parents, CHILD * rows, rank), BF16),
            pltpu.VMEM((parents, rank, CHILD * rows), BF16),
            pltpu.VMEM((leaves + 2 * NWIN, rows * nk, vectors), BF16),
            pltpu.VMEM((leaves + 2 * NWIN, rows * nk, vectors), BF16),
            pltpu.VMEM((chunks, 3 * NWIN, NWIN * rows, near_blocks.shape[3]), BF16),
            pltpu.VMEM((2, nk, parents, share, vectors), BF16),
            pltpu.VMEM((2, nk, parents, share, vectors), BF16),
            *[pltpu.VMEM((nc * parents, share, vectors // 2), BF16)] * 4,
            pltpu.VMEM((2, parents, rank, vectors), BF16),
            pltpu.VMEM((2, nk, parents, rank, vectors), BF16),
            pltpu.VMEM((chunks, NWIN * rows, vectors), F32),
            dma((7,)),
            dma,
            dma((2, nk, chunks)),
            dma((2, nk, chunks)),
            dma((2, 2, nk)),
            dma((2, 2, nk)),
            dma((2, 2, nk)),
            dma((2, 2, nk)),
            dma((2, 2, 2, outer)),
            dma((2, 2, 2, outer)),
            dma((2, 2, 2, outer)),
            dma((2, 2, 2, outer)),
            dma((2, 2, nk)),
            dma((2, 2, nk)),
        ],
        compiler_params=pltpu.CompilerParams(
            collective_id=0, has_side_effects=True, vmem_limit_bytes=56 * 1024 * 1024
        ),
        cost_estimate=pl.CostEstimate(
            flops=4 * near_blocks.size * vectors, bytes_accessed=2 * near_blocks.size,
            transcendentals=0,
        ),
    )(density, near_list, far_list, near_blocks, basis, transfer, coupling)
    return pl.pallas_call(
        functools.partial(hand_over, chunks // 2),
        out_shape=(jax.ShapeDtypeStruct(density.shape, BF16),) * 2,
        in_specs=[anywhere] * 2,
        out_specs=(anywhere,) * 2,
        scratch_shapes=[
            pltpu.VMEM((2,) + density.shape, BF16), dma((2, chunks)), dma((2, chunks)),
        ],
        compiler_params=pltpu.CompilerParams(vmem_limit_bytes=56 * 1024 * 1024),
    )(*held)


def solution(mesh):
    placed = (
        P("clus", "coef", None),
        P("clus", None),
        P("clus", None),
        P("clus", None, "coef", None),
        P("clus", "coef", None),
        P("clus", None, None),
        P("clus", None, None, "coef"),
    )
    return jax.shard_map(
        functools.partial(body, mesh.shape["clus"], mesh.shape["coef"]),
        mesh=mesh,
        in_specs=placed,
        out_specs=(P("clus", "coef", None), P("clus", "coef", None)),
        check_vma=False,
    )
```
